32 devices in a mesh: dp: 16 (over z, y, x), tensor: 2 (over core).
Axes of the slice: x: 2, y: 2, z: 4, core: 2. Of those that a mesh axis runs over, the one named last changes fastest.
Arguments:
- grad_kv: bfloat16 [16, 2, 512, 2048], P('dp', None, 'tensor'), may hold values from -6 to 6
- error_kv: bfloat16 [16, 2, 512, 2048], P('dp', None, 'tensor'), may hold values from -4 to 4
- moment_kv: bfloat16 [16, 2, 512, 2048], P('dp', None, 'tensor'), may hold values from -6 to 6
- start_dirs: float32 [2, 32, 2048], replicated, may hold values from -6 to 6
- weight_kv: float32 [2, 512, 2048], P(None, 'tensor', 'dp'), may hold values from -6 to 6
- norm_grads: bfloat16 [16, 2, 2048], P('dp', None, 'tensor'), may hold values from -6 to 6
- norm_gains: float32 [2, 2, 1024], P(None, 'tensor', 'dp'), may hold values from 0.5 to 1.5
Outputs:
- new_weight_kv: float32 [2, 512, 2048], P(None, 'tensor', 'dp')
- new_error_kv: bfloat16 [16, 2, 512, 2048], P('dp', None, 'tensor')
- new_moment_kv: bfloat16 [16, 2, 512, 2048], P('dp', None, 'tensor')
- new_gains: float32 [2, 2, 1024], P(None, 'tensor', 'dp')
The draws below stay inside these ranges and needn't reach their ends.
All inputs are finite; a program needn't handle non-finite values.
Results may differ from the reference program's by a relative error of at most 0.001.
Values sent between devices are 32-bit elements; how exact they have to be, the bound alone decides.
A program may use at most 64 MiB of HBM per device.

```python
import jax
import jax.numpy as jnp
from jax import lax

D = 2048
KVW = 512
RANK = 32
ROUNDS = 2
REPLICAS = 16
N_TENSOR = 2


def spiked(result, stream_key, source, target, blocks, factor):
    owner, partner = [(jnp.arange(result.shape[position]) // (result.shape[position] // blocks)).reshape([-1 if axis == position else 1 for axis in range(result.ndim)]) for position in (source, target)]
    chosen = jax.random.permutation(stream_key, blocks)[partner]
    strong = (owner == chosen) | (owner == (partner + blocks // 2) % blocks)
    return jnp.where(strong, factor * result, result)


def steps_of(rng, extent, pieces, smallest, high):
    gain, own = 1.0, jax.random.fold_in(rng, 6)
    for dim, blocks in pieces:
        draws = jnp.exp(jax.random.uniform(jax.random.fold_in(own, dim), (blocks,), jnp.float32, smallest / len(pieces), high / len(pieces)))
        gain = gain * jnp.repeat(draws, extent[dim] // blocks).reshape([-1 if axis == dim else 1 for axis in range(len(extent))])
    return gain


def bell_draw(rng, dims, deviation, reach, pieces=(), kind=jnp.bfloat16):
    result = jax.random.normal(rng, dims, jnp.float32) * deviation
    if len(pieces) > 0:
        result = steps_of(rng, dims, pieces, -0.22, 0.18) * result
    return jnp.clip(result, min=-reach, max=reach).astype(kind)


def gaussian_with(rng, extent, deviation, reach, cuts, heavy, kind=jnp.bfloat16):
    drawn = deviation * jax.random.normal(rng, extent, jnp.float32)
    if cuts:
        drawn = drawn * steps_of(rng, extent, cuts, -0.22, 0.18)
    return jnp.clip(spiked(drawn, jax.random.fold_in(rng, 3), *heavy), -reach, reach).astype(kind)


def setup_inputs(seed: int = 0) -> dict:
    arg_keys = jax.random.split(jax.random.key(seed), 8)
    return {
        "grad_kv": gaussian_with(arg_keys[0], (REPLICAS, 2, KVW, D), 1.0, 6.0, ((0, 16), (2, 2)), (0, 3, 16, 2.0)),
        "error_kv": bell_draw(arg_keys[1], (REPLICAS, 2, KVW, D), 0.5, 4.0, ((0, 16), (2, 2))),
        "moment_kv": bell_draw(arg_keys[2], (REPLICAS, 2, KVW, D), 1.0, 6.0, ((0, 16), (2, 2))),
        "start_dirs": bell_draw(arg_keys[3], (2, RANK, D), 1.0, 6.0, (), jnp.float32),
        "weight_kv": bell_draw(arg_keys[4], (2, KVW, D), 1.0, 6.0, ((1, 2), (2, 16)), jnp.float32),
        "norm_grads": gaussian_with(arg_keys[5], (REPLICAS, 2, D), 1.0, 6.0, ((0, 16), (2, 2)), (0, 2, 16, 2.0)),
        "norm_gains": jnp.clip(1.0 + 0.1 * jax.random.normal(arg_keys[6], (2, N_TENSOR, D // N_TENSOR), jnp.float32), 0.5, 1.5),
    }


momentum_decay = 0.9
step_size = 0.5

def tri_solve(triangle, columns):
    return jax.scipy.linalg.solve_triangular(triangle, columns, lower=True)

def orthonormal(factor):
    gram_matrix = jnp.einsum('mrk,mrj->mkj', factor, factor, precision=lax.Precision.HIGHEST)
    cholesky_factor = jnp.linalg.cholesky(gram_matrix)
    solved = jax.vmap(tri_solve)(cholesky_factor, jnp.swapaxes(factor, 1, 2))
    return jnp.swapaxes(solved, 1, 2)

def reference(grad_kv, error_kv, moment_kv, start_dirs, weight_kv, norm_grads, norm_gains):
    moment_f = momentum_decay * moment_kv.astype(jnp.float32) + grad_kv.astype(jnp.float32)
    new_moment_kv = moment_f.astype(jnp.bfloat16)
    inputs = moment_f + error_kv.astype(jnp.float32)
    directions = start_dirs.astype(jnp.float32)
    basis = None
    for step in range(ROUNDS):
        factor = jnp.einsum('nmrd,mkd->mrk', inputs, directions, precision=lax.Precision.HIGHEST)
        basis = orthonormal(factor)
        directions = jnp.einsum('nmrd,mrk->mkd', inputs, basis, precision=lax.Precision.HIGHEST)
    approx = jnp.einsum('mrk,mkd->mrd', basis, directions, precision=lax.Precision.HIGHEST) / REPLICAS
    new_error_kv = (inputs - approx[None]).astype(jnp.bfloat16)
    new_weight_kv = weight_kv - step_size * approx
    mean_norm = jnp.sum(norm_grads.astype(jnp.float32), axis=0) / REPLICAS
    gains_flat = norm_gains.reshape(2, D)
    new_gains = (gains_flat - step_size * mean_norm).reshape(2, N_TENSOR, D // N_TENSOR)
    return (new_weight_kv, new_error_kv, new_moment_kv, new_gains)
```

```python
import functools

import jax
import jax.numpy as jnp
from jax import lax
from jax.experimental import pallas as pl
from jax.experimental.pallas import tpu as pltpu
from jax.sharding import PartitionSpec as P

momentum_decay = 0.9
step_size = 0.5
LANES = 128
SUBLANES = 8
F32 = jnp.float32
BF16 = jnp.bfloat16
HIGHEST = lax.Precision.HIGHEST


def project(inputs, directions):
    return jnp.einsum("mrd,mkd->mrk", inputs, directions, precision=HIGHEST)


def tri_solve(triangle, columns):
    return jax.scipy.linalg.solve_triangular(triangle, columns, lower=True)


def orthonormal(factor):
    full_rows = lax.all_gather(factor, "tensor", axis=1, tiled=True)
    gram_matrix = jnp.einsum("mrk,mrj->mkj", full_rows, full_rows, precision=HIGHEST)
    cholesky_factor = jnp.linalg.cholesky(gram_matrix)
    solved = jax.vmap(tri_solve)(cholesky_factor, jnp.swapaxes(factor, 1, 2))
    return jnp.swapaxes(solved, 1, 2)


def column_sums(inputs, basis):
    partial_sum = jnp.einsum("mrd,mrk->mkd", inputs, basis, precision=HIGHEST)
    return lax.psum(partial_sum, ("dp", "tensor"))


def plain_shards(grad_kv, error_kv, moment_kv, start_dirs, weight_kv, norm_grads, norm_gains):
    replicas = lax.axis_size("dp")
    dp_index = lax.axis_index("dp")
    moment_f = momentum_decay * moment_kv.astype(F32) + grad_kv.astype(F32)
    new_moment_kv = moment_f.astype(BF16)
    inputs = (moment_f + error_kv.astype(F32))[0]
    norm_terms = norm_grads[0].astype(F32)
    gain_cols = norm_gains.shape[2]
    factor = project(inputs, start_dirs)
    factor, norm_total = lax.psum((factor, norm_terms), "dp")
    own_norm = lax.dynamic_slice_in_dim(norm_total, dp_index * gain_cols, gain_cols, 1)
    mean_norm = own_norm / replicas
    basis = orthonormal(factor)
    directions = column_sums(inputs, basis)
    factor = lax.psum(project(inputs, directions), "dp")
    basis = orthonormal(factor)
    directions = column_sums(inputs, basis)
    approx = jnp.einsum("mrk,mkd->mrd", basis, directions, precision=HIGHEST) / replicas
    new_error_kv = (inputs - approx).astype(BF16)[None]
    weight_cols = weight_kv.shape[2]
    own_approx = lax.dynamic_slice_in_dim(approx, dp_index * weight_cols, weight_cols, 2)
    new_weight_kv = weight_kv - step_size * own_approx
    new_gains = norm_gains - step_size * mean_norm[:, None, :]
    return (new_weight_kv, new_error_kv, new_moment_kv, new_gains)


def split(value):
    high = value.astype(BF16)
    return high, (value - high.astype(F32)).astype(BF16)


def dot_nt(a, b):
    return lax.dot_general(a, b, (((1,), (1,)), ((), ())), preferred_element_type=F32)


def dot_tn(a, b):
    return lax.dot_general(a, b, (((0,), (0,)), ((), ())), preferred_element_type=F32)


def basis_of(factor, block=4):
    rank = factor.shape[0]
    gram = lax.dot_general(
        factor, factor, (((1,), (1,)), ((), ())), precision=HIGHEST, preferred_element_type=F32
    )
    row_id = lax.broadcasted_iota(jnp.int32, (rank, 2 * rank), 0)
    col_id = lax.broadcasted_iota(jnp.int32, (rank, 2 * rank), 1)
    unit = (lax.broadcasted_iota(jnp.int32, (rank, rank), 0) == lax.broadcasted_iota(jnp.int32, (rank, rank), 1)).astype(F32)
    work = jnp.concatenate([gram, unit], axis=1)
    for first in range(0, rank, block):
        cols = [jnp.broadcast_to(work[:, j : j + 1], work.shape) for j in range(first, first + block)]
        rows = [work[j : j + 1, :] for j in range(first, first + block)]
        for i in range(block):
            j = first + i
            ratio = jnp.where(row_id > j, cols[i] / cols[i][j : j + 1, :], 0.0)
            for k in range(i + 1, block):
                cols[k] = cols[k] - ratio * cols[k][j : j + 1, :]
                rows[k] = rows[k] - ratio[first + k : first + k + 1, :] * rows[i]
            work = work - ratio * rows[i]
    pivots = jnp.sum(jnp.where(row_id == col_id, work, 0.0), axis=1, keepdims=True)
    inverse = work[:, rank:] * lax.rsqrt(pivots)
    return jnp.dot(inverse, factor, precision=HIGHEST, preferred_element_type=F32)


def kernel(
    replicas, chunks,
    grad, error, moment, start_dirs, weight, norm_grads, gains,
    new_weight, new_error, new_moment, new_gains,
    grad_in, error_in, moment_in, dirs_in, moment_out, error_out, inputs, swapped, high, low,
    norm_send, norm_recv, factor_send, factor_recv, factor_all, dirs_send, dirs_recv, dirs_all,
    basis_own, basis_other, dirs_other,
    load_sem, store_sem, swap_send, swap_recv, norm_ssem, norm_rsem,
    fs_ssem, fs_rsem, fg_ssem, fg_rsem, ds_ssem, ds_rsem, dg_ssem, dg_rsem,
):
    me, core = lax.axis_index("dp"), lax.axis_index("tensor")
    other = 1 - core
    rows, width = inputs.shape[1:]
    rank = dirs_in.shape[0]
    piece_rows = rows // chunks

    def remote(src, dst, send_sem, recv_sem, to):
        return pltpu.make_async_remote_copy(
            src_ref=src, dst_ref=dst, send_sem=send_sem, recv_sem=recv_sem,
            device_id=to, device_id_type=pl.DeviceIdType.MESH,
        )

    def each_peer(body):
        def step(d, carry):
            body(d, lax.rem(me + d, replicas), lax.rem(me + replicas - d, replicas))
            return carry
        lax.fori_loop(1, replicas, step, 0)

    def scatter(send, recv, ssem, rsem):
        return lambda d, to, frm: remote(send.at[to], recv.at[d - 1], ssem.at[d - 1], rsem.at[d - 1], (to, core))

    def gather(full, ssem, rsem, receive=False):
        def copy(d, to, frm):
            slot = full.at[frm] if receive else full.at[me]
            return remote(slot, slot, ssem.at[d - 1], rsem.at[d - 1], (to, core))
        return copy

    def start(make):
        each_peer(lambda *a: make(*a).start())

    def wait_recv(make):
        each_peer(lambda *a: make(*a).wait_recv())

    def wait_send(make):
        each_peer(lambda *a: make(*a).wait_send())

    dirs_copy = pltpu.make_async_copy(start_dirs.at[core], dirs_in, load_sem.at[6 * chunks])
    loads = []
    for i, m in enumerate((other, core)):
        for c in range(chunks):
            r = pl.ds(c * piece_rows, piece_rows)
            loads.append([
                pltpu.make_async_copy(src.at[0, m, r], dst.at[m, r], load_sem.at[(i * chunks + c) * 3 + k])
                for k, (src, dst) in enumerate(((grad, grad_in), (moment, moment_in), (error, error_in)))
            ])
    for group in loads:
        for copy in group:
            copy.start()
    dirs_copy.start()

    barrier = pltpu.get_barrier_semaphore()
    each_peer(lambda d, to, frm: pl.semaphore_signal(
        barrier, inc=1, device_id=(to, core), device_id_type=pl.DeviceIdType.MESH))
    pl.semaphore_signal(barrier, inc=1, device_id=(me, other), device_id_type=pl.DeviceIdType.MESH)

    gain_cols = gains.shape[2]
    terms = norm_grads[0].astype(F32)
    for p in range(replicas):
        norm_send[p] = terms[:, p * gain_cols : (p + 1) * gain_cols]
    pl.semaphore_wait(barrier, replicas)

    swaps, stores = [], []
    for i, m in enumerate((other, core)):
        for c in range(chunks):
            for copy in loads[i * chunks + c]:
                copy.wait()

            @pl.loop(0, piece_rows // 16)
            def _(g):
                r = pl.ds(pl.multiple_of(c * piece_rows + g * 16, 16), 16)
                moment_f = momentum_decay * moment_in[m, r, :].astype(F32) + grad_in[m, r, :].astype(F32)
                moment_out[m, r, :] = moment_f.astype(BF16)
                x = moment_f + error_in[m, r, :].astype(F32)
                inputs[m, r, :] = x
                if i == 1:
                    high[core, r, :], low[core, r, :] = split(x)

            r = pl.ds(c * piece_rows, piece_rows)
            if i == 0:
                swaps.append(remote(inputs.at[m, r], swapped.at[r], swap_send.at[c], swap_recv.at[c], (me, other)))
                swaps[-1].start()
            stores.append(pltpu.make_async_copy(moment_out.at[m, r], new_moment.at[0, m, r], store_sem.at[i * chunks + c]))
            stores[-1].start()
    norm_copies = scatter(norm_send, norm_recv, norm_ssem, norm_rsem)
    start(norm_copies)
    dirs_copy.wait()
    for c in range(chunks):
        swaps[c].wait_recv()

        @pl.loop(0, piece_rows // 16)
        def _(g):
            r = pl.ds(pl.multiple_of(c * piece_rows + g * 16, 16), 16)
            high[other, r, :], low[other, r, :] = split(swapped[r, :])

    row_blocks = 2 * rows // LANES
    tiles = [(a, b) for a in range(rank // SUBLANES) for b in range(row_blocks)]

    def left(step, dirs):
        dirs_high, dirs_low = split(dirs)
        both = jnp.concatenate([dirs_high, dirs_low], axis=0)
        halves = []
        for h in range(2):
            part = dot_nt(both, high[h])
            halves.append(part[:rank] + part[rank:] + dot_nt(dirs_high, low[h]))
        factor = jnp.concatenate(halves, axis=1)
        send, recv, full = factor_send.at[step], factor_recv.at[step], factor_all.at[step]
        for j, (a, b) in enumerate(tiles):
            send[j] = factor[a * SUBLANES : (a + 1) * SUBLANES, b * LANES : (b + 1) * LANES]
        out = scatter(send, recv, fs_ssem.at[step], fs_rsem.at[step])
        start(out)
        wait_recv(out)
        total = send[me]
        for d in range(replicas - 1):
            total = total + recv[d]
        full[me] = total
        start(gather(full, fg_ssem.at[step], fg_rsem.at[step]))
        wait_recv(gather(full, fg_ssem.at[step], fg_rsem.at[step], True))
        return jnp.concatenate(
            [jnp.concatenate([full[a * row_blocks + b] for b in range(row_blocks)], axis=1) for a in range(rank // SUBLANES)],
            axis=0,
        )

    def right(step, basis):
        basis_high, basis_low = split(basis)
        both = jnp.concatenate([basis_high, basis_low], axis=0)
        send, recv, full = dirs_send.at[step], dirs_recv.at[step], dirs_all.at[step]
        span = min(width, 4 * LANES)
        for first in range(0, width, span):
            part = low_part = 0.0
            for h in range(2):
                part += jnp.dot(both[:, h * rows : (h + 1) * rows], high[h, :, first : first + span], preferred_element_type=F32)
                low_part += jnp.dot(basis_high[:, h * rows : (h + 1) * rows], low[h, :, first : first + span], preferred_element_type=F32)
            block = part[:rank] + part[rank:] + low_part
            for j in range(span // LANES):
                send[first // LANES + j] = block[:, j * LANES : (j + 1) * LANES]
        out = scatter(send, recv, ds_ssem.at[step], ds_rsem.at[step])
        start(out)
        wait_recv(out)
        total = send[me]
        for d in range(replicas - 1):
            total = total + recv[d]
        full[me] = total
        start(gather(full, dg_ssem.at[step], dg_rsem.at[step]))
        wait_recv(gather(full, dg_ssem.at[step], dg_rsem.at[step], True))

    right(0, basis_of(left(0, dirs_in[...])))
    full_dirs = jnp.concatenate([dirs_all[0, p] for p in range(replicas)], axis=1)
    basis = basis_of(left(1, full_dirs))
    basis_own[0], basis_own[1] = basis[:, :rows], basis[:, rows:]
    basis_swap = remote(basis_own.at[other], basis_other, swap_send.at[chunks], swap_recv.at[chunks], (me, other))
    basis_swap.start()
    right(1, basis)
    dirs_swap = remote(dirs_all.at[1], dirs_other, swap_send.at[chunks + 1], swap_recv.at[chunks + 1], (me, other))
    dirs_swap.start()

    def finish(m, basis_half, dirs):
        basis_high, basis_low = split(basis_half)
        lhs = jnp.concatenate([basis_high, basis_high, basis_low], axis=0)

        def approx_of(block):
            dirs_high, dirs_low = split(block)
            return dot_tn(lhs, jnp.concatenate([dirs_high, dirs_low, dirs_high], axis=0)) / replicas

        for first in range(0, replicas, 2):
            cols = slice(first * LANES, (first + 2) * LANES)
            approx = approx_of(jnp.concatenate([dirs[first], dirs[first + 1]], axis=1))
            error_out[m, :, cols] = (inputs[m, :, cols] - approx).astype(BF16)
        new_weight[m] = weight[m] - step_size * approx_of(dirs[me])

    def store_error(i, m):
        copy = pltpu.make_async_copy(error_out.at[m], new_error.at[0, m], store_sem.at[2 * chunks + i])
        copy.start()
        stores.append(copy)

    finish(core, basis_own[core], dirs_all.at[1])
    store_error(0, core)
    wait_recv(norm_copies)
    total = norm_send[me]
    for d in range(replicas - 1):
        total = total + norm_recv[d]
    for m in range(2):
        new_gains[m] = gains[m] - step_size * (total[m : m + 1] / replicas)
    basis_swap.wait_recv()
    dirs_swap.wait_recv()
    finish(other, basis_other[...], dirs_other)
    store_error(1, other)

    for copy in swaps + [basis_swap, dirs_swap]:
        copy.wait_send()
    wait_send(norm_copies)
    for s in range(2):
        wait_send(scatter(factor_send.at[s], factor_recv.at[s], fs_ssem.at[s], fs_rsem.at[s]))
        wait_send(gather(factor_all.at[s], fg_ssem.at[s], fg_rsem.at[s]))
        wait_send(scatter(dirs_send.at[s], dirs_recv.at[s], ds_ssem.at[s], ds_rsem.at[s]))
        wait_send(gather(dirs_all.at[s], dg_ssem.at[s], dg_rsem.at[s]))
    for copy in stores:
        copy.wait()


def kernel_shards(grad_kv, error_kv, moment_kv, start_dirs, weight_kv, norm_grads, norm_gains):
    replicas = lax.axis_size("dp")
    _, matrices, rows, width = grad_kv.shape
    rank = start_dirs.shape[1]
    gain_cols = norm_gains.shape[2]
    chunks = 2
    near = replicas - 1
    any_spec, vmem = pl.BlockSpec(memory_space=pl.ANY), pl.BlockSpec(memory_space=pltpu.VMEM)
    whole = (matrices, rows, width)
    dma = pltpu.SemaphoreType.DMA
    return pl.pallas_call(
        functools.partial(kernel, replicas, chunks),
        out_shape=(
            jax.ShapeDtypeStruct(weight_kv.shape, F32),
            jax.ShapeDtypeStruct(error_kv.shape, BF16),
            jax.ShapeDtypeStruct(moment_kv.shape, BF16),
            jax.ShapeDtypeStruct(norm_gains.shape, F32),
        ),
        in_specs=[any_spec] * 4 + [vmem] * 3,
        out_specs=(vmem, any_spec, any_spec, vmem),
        scratch_shapes=[
            pltpu.VMEM(whole, BF16), pltpu.VMEM(whole, BF16), pltpu.VMEM(whole, BF16),
            pltpu.VMEM((rank, width), F32), pltpu.VMEM(whole, BF16), pltpu.VMEM(whole, BF16),
            pltpu.VMEM(whole, F32), pltpu.VMEM((rows, width), F32),
            pltpu.VMEM(whole, BF16), pltpu.VMEM(whole, BF16),
            pltpu.VMEM((replicas, matrices, gain_cols), F32), pltpu.VMEM((near, matrices, gain_cols), F32),
            pltpu.VMEM((2, replicas, SUBLANES, LANES), F32), pltpu.VMEM((2, near, SUBLANES, LANES), F32),
            pltpu.VMEM((2, replicas, SUBLANES, LANES), F32),
            pltpu.VMEM((2, replicas, rank, LANES), F32), pltpu.VMEM((2, near, rank, LANES), F32),
            pltpu.VMEM((2, replicas, rank, LANES), F32),
            pltpu.VMEM((2, rank, rows), F32), pltpu.VMEM((rank, rows), F32),
            pltpu.VMEM((replicas, rank, LANES), F32),
            dma((6 * chunks + 1,)), dma((2 * chunks + 2,)), dma((chunks + 2,)), dma((chunks + 2,)),
            dma((near,)), dma((near,)),
        ] + [dma((2, near))] * 8,
        compiler_params=pltpu.CompilerParams(
            collective_id=0, has_side_effects=True, vmem_limit_bytes=44 * 2**20
        ),
        name="power_step",
    )(grad_kv, error_kv, moment_kv, start_dirs, weight_kv, norm_grads, norm_gains)


def solution(mesh):
    replicas, tensor = mesh.shape["dp"], mesh.shape["tensor"]

    def shards(*args):
        _, matrices, rows, width = args[0].shape
        rank = args[3].shape[1]
        fits = (
            tensor == matrices == 2
            and width == LANES * replicas
            and (rank // SUBLANES) * (2 * rows // LANES) == replicas
            and rank % SUBLANES == 0
            and rows % (2 * LANES) == 0
            and replicas % 2 == 0
        )
        return (kernel_shards if fits else plain_shards)(*args)

    return jax.shard_map(
        shards,
        mesh=mesh,
        in_specs=(
            P("dp", None, "tensor", None),
            P("dp", None, "tensor", None),
            P("dp", None, "tensor", None),
            P(),
            P(None, "tensor", "dp"),
            P("dp", None, "tensor"),
            P(None, "tensor", "dp"),
        ),
        out_specs=(
            P(None, "tensor", "dp"),
            P("dp", None, "tensor", None),
            P("dp", None, "tensor", None),
            P(None, "tensor", "dp"),
        ),
        check_vma=False,
    )
```

```python
import functools

import jax
import jax.numpy as jnp
from jax import lax
from jax.experimental import pallas as pl
from jax.experimental.pallas import tpu as pltpu
from jax.sharding import PartitionSpec as P

momentum_decay = 0.9
step_size = 0.5
LANES = 128
SUBLANES = 8
F32 = jnp.float32
BF16 = jnp.bfloat16
HIGHEST = lax.Precision.HIGHEST


def project(inputs, directions):
    return jnp.einsum("mrd,mkd->mrk", inputs, directions, precision=HIGHEST)


def tri_solve(triangle, columns):
    return jax.scipy.linalg.solve_triangular(triangle, columns, lower=True)


def orthonormal(factor):
    full_rows = lax.all_gather(factor, "tensor", axis=1, tiled=True)
    gram_matrix = jnp.einsum("mrk,mrj->mkj", full_rows, full_rows, precision=HIGHEST)
    cholesky_factor = jnp.linalg.cholesky(gram_matrix)
    solved = jax.vmap(tri_solve)(cholesky_factor, jnp.swapaxes(factor, 1, 2))
    return jnp.swapaxes(solved, 1, 2)


def column_sums(inputs, basis):
    partial_sum = jnp.einsum("mrd,mrk->mkd", inputs, basis, precision=HIGHEST)
    return lax.psum(partial_sum, ("dp", "tensor"))


def plain_shards(grad_kv, error_kv, moment_kv, start_dirs, weight_kv, norm_grads, norm_gains):
    replicas = lax.axis_size("dp")
    dp_index = lax.axis_index("dp")
    moment_f = momentum_decay * moment_kv.astype(F32) + grad_kv.astype(F32)
    new_moment_kv = moment_f.astype(BF16)
    inputs = (moment_f + error_kv.astype(F32))[0]
    norm_terms = norm_grads[0].astype(F32)
    gain_cols = norm_gains.shape[2]
    factor = project(inputs, start_dirs)
    factor, norm_total = lax.psum((factor, norm_terms), "dp")
    own_norm = lax.dynamic_slice_in_dim(norm_total, dp_index * gain_cols, gain_cols, 1)
    mean_norm = own_norm / replicas
    basis = orthonormal(factor)
    directions = column_sums(inputs, basis)
    factor = lax.psum(project(inputs, directions), "dp")
    basis = orthonormal(factor)
    directions = column_sums(inputs, basis)
    approx = jnp.einsum("mrk,mkd->mrd", basis, directions, precision=HIGHEST) / replicas
    new_error_kv = (inputs - approx).astype(BF16)[None]
    weight_cols = weight_kv.shape[2]
    own_approx = lax.dynamic_slice_in_dim(approx, dp_index * weight_cols, weight_cols, 2)
    new_weight_kv = weight_kv - step_size * own_approx
    new_gains = norm_gains - step_size * mean_norm[:, None, :]
    return (new_weight_kv, new_error_kv, new_moment_kv, new_gains)


def split(value):
    high = value.astype(BF16)
    return high, (value - high.astype(F32)).astype(BF16)


def dot_nt(a, b):
    return lax.dot_general(a, b, (((1,), (1,)), ((), ())), preferred_element_type=F32)


def dot_tn(a, b):
    return lax.dot_general(a, b, (((0,), (0,)), ((), ())), preferred_element_type=F32)


def basis_of(factor, block=8):
    rank = factor.shape[0]
    gram = lax.dot_general(
        factor, factor, (((1,), (1,)), ((), ())), precision=HIGHEST, preferred_element_type=F32
    )
    row_id = lax.broadcasted_iota(jnp.int32, (rank, 2 * rank), 0)
    col_id = lax.broadcasted_iota(jnp.int32, (rank, 2 * rank), 1)
    unit = (lax.broadcasted_iota(jnp.int32, (rank, rank), 0) == lax.broadcasted_iota(jnp.int32, (rank, rank), 1)).astype(F32)
    work = jnp.concatenate([gram, unit], axis=1)
    for first in range(0, rank, block):
        cols = [jnp.broadcast_to(work[:, j : j + 1], work.shape) for j in range(first, first + block)]
        rows = [work[j : j + 1, :] for j in range(first, first + block)]
        for i in range(block):
            j = first + i
            ratio = jnp.where(row_id > j, cols[i] / cols[i][j : j + 1, :], 0.0)
            for k in range(i + 1, block):
                cols[k] = cols[k] - ratio * cols[k][j : j + 1, :]
                rows[k] = rows[k] - ratio[first + k : first + k + 1, :] * rows[i]
            work = work - ratio * rows[i]
    pivots = jnp.sum(jnp.where(row_id == col_id, work, 0.0), axis=1, keepdims=True)
    inverse = work[:, rank:] * lax.rsqrt(pivots)
    return jnp.dot(inverse, factor, precision=HIGHEST, preferred_element_type=F32)


def kernel(
    outer, inner, chunks,
    grad, error, moment, start_dirs, weight, norm_grads, gains,
    new_weight, new_error, new_moment, new_gains,
    grad_in, error_in, moment_in, dirs_in, weight_in, norm_in, gains_in, inputs, swapped, high, low,
    norm_send, norm_recv, norm_part, norm_far,
    first_send, first_recv, factor_send, factor_near, factor_far, factor_all,
    dirs_send, dirs_near, dirs_part, dirs_far, dirs_all, basis_own, basis_other, dirs_other,
    load_sem, swap_ssem, swap_rsem, norm_ssem, norm_rsem, factor_ssem, factor_rsem, dirs_ssem, dirs_rsem,
):
    me, core = lax.axis_index("dp"), lax.axis_index("tensor")
    other = 1 - core
    far, near = lax.div(me, inner), lax.rem(me, inner)
    replicas = outer * inner
    rows, width = inputs.shape[1:]
    rank = dirs_in.shape[1]
    piece_rows = rows // chunks
    span = width // outer
    sends = []

    def remote(src, dst, send_sem, recv_sem, to):
        return pltpu.make_async_remote_copy(
            src_ref=src, dst_ref=dst, send_sem=send_sem, recv_sem=recv_sem,
            device_id=to, device_id_type=pl.DeviceIdType.MESH,
        )

    def send(*args):
        copy = remote(*args)
        copy.start()
        sends.append(copy)
        return copy

    def near_at(d):
        return lax.rem(near + d + inner, inner)

    def far_at(d):
        return lax.rem(far + d + outer, outer)

    def near_peer(d):
        return (far * inner + near_at(d), core)

    def far_peer(d):
        return (far_at(d) * inner + near, core)

    def columns(z):
        return pl.ds(pl.multiple_of(z * span, span), span)

    last = 6 * chunks
    small = [
        pltpu.make_async_copy(src, dst, load_sem.at[last + k])
        for k, (src, dst) in enumerate(((start_dirs, dirs_in), (norm_grads, norm_in), (weight, weight_in), (gains, gains_in)))
    ]
    loads = []
    for i, m in enumerate((other, core)):
        for c in range(chunks):
            r = pl.ds(c * piece_rows, piece_rows)
            loads.append([
                pltpu.make_async_copy(src.at[0, m, r], dst.at[m, r], load_sem.at[(i * chunks + c) * 3 + k])
                for k, (src, dst) in enumerate(((grad, grad_in), (moment, moment_in), (error, error_in)))
            ])
    for n, group in enumerate(loads):
        for copy in group:
            copy.start()
        if n == 0:
            small[0].start()
            small[1].start()
    small[2].start()
    small[3].start()

    barrier = pltpu.get_barrier_semaphore()
    greeted = [near_peer(d) for d in range(1, inner)] + [far_peer(d) for d in range(1, outer)] + [(me, other)]
    for device in greeted:
        pl.semaphore_signal(barrier, inc=1, device_id=device, device_id_type=pl.DeviceIdType.MESH)

    def form(i, m):
        for c in range(chunks):
            for copy in loads[i * chunks + c]:
                copy.wait()

            @pl.loop(0, piece_rows // 16)
            def _(g):
                r = pl.ds(pl.multiple_of(c * piece_rows + g * 16, 16), 16)
                moment_f = momentum_decay * moment_in[m, r, :].astype(F32) + grad_in[m, r, :].astype(F32)
                new_moment[0, m, r, :] = moment_f.astype(BF16)
                x = moment_f + error_in[m, r, :].astype(F32)
                inputs[m, r, :] = x
                high[m, r, :], low[m, r, :] = split(x)

    def left_of(dirs, h, cols=slice(None)):
        dirs_high, dirs_low = split(dirs)
        part = dot_nt(jnp.concatenate([dirs_high, dirs_low], axis=0), high[h, :, cols])
        return part[:rank] + part[rank:] + dot_nt(dirs_high, low[h, :, cols])

    def left_sum(step, factor, between=None):
        block = rank // inner
        own, arrived, summed, full = factor_send.at[step], factor_near.at[step], factor_far.at[step], factor_all.at[step]
        ssem, rsem = factor_ssem.at[step], factor_rsem.at[step]
        for q in range(inner):
            own[q] = factor[q * block : (q + 1) * block, :]
        waits = [send(own.at[near_at(d)], arrived.at[d - 1], ssem.at[d - 1], rsem.at[d - 1], near_peer(d)) for d in range(1, inner)]
        if between is not None:
            between()
        total = own[near]
        for d in range(1, inner):
            waits[d - 1].wait_recv()
            total = total + arrived[d - 1]
        summed[far] = total
        base = inner - 1
        for d in range(1, outer):
            send(summed.at[far], summed.at[far], ssem.at[base + d - 1], rsem.at[base + d - 1], far_peer(d))
        for d in range(1, outer):
            slot = summed.at[far_at(-d)]
            remote(slot, slot, ssem.at[base + d - 1], rsem.at[base + d - 1], far_peer(d)).wait_recv()
        total = summed[0]
        for z in range(1, outer):
            total = total + summed[z]
        full[near] = total
        base += outer - 1
        for d in range(1, inner):
            send(full.at[near], full.at[near], ssem.at[base + d - 1], rsem.at[base + d - 1], near_peer(d))
        for d in range(1, inner):
            slot = full.at[near_at(-d)]
            remote(slot, slot, ssem.at[base + d - 1], rsem.at[base + d - 1], near_peer(d)).wait_recv()
        return jnp.concatenate([full[q] for q in range(inner)], axis=0)

    def right_sum(step, basis, consume):
        basis_high, basis_low = split(basis)
        both = jnp.concatenate([basis_high, basis_low], axis=0)
        own, arrived, part, other_far, full = (
            dirs_send.at[step], dirs_near.at[step], dirs_part.at[step], dirs_far.at[step], dirs_all.at[step]
        )
        ssem, rsem = dirs_ssem.at[step], dirs_rsem.at[step]
        order = list(range(1, outer)) + [0]
        waits = {}
        for dz in order:
            z = far_at(dz)
            sums = low_sums = 0.0
            for h in range(2):
                half = slice(h * rows, (h + 1) * rows)
                sums += jnp.dot(both[:, half], high[h, :, columns(z)], preferred_element_type=F32)
                low_sums += jnp.dot(basis_high[:, half], low[h, :, columns(z)], preferred_element_type=F32)
            block = sums[:rank] + sums[rank:] + low_sums
            for q in range(inner):
                own[z, q] = block[:, q * LANES : (q + 1) * LANES]
            for d in range(1, inner):
                k = dz * (inner - 1) + d - 1
                waits[dz, d] = send(own.at[z, near_at(d)], arrived.at[z, d - 1], ssem.at[k], rsem.at[k], near_peer(d))
        base = outer * (inner - 1)
        far_waits = []
        for dz in order:
            z = far_at(dz)
            total = own[z, near]
            for d in range(1, inner):
                waits[dz, d].wait_recv()
                total = total + arrived[z, d - 1]
            if dz:
                part[z] = total
                k = base + dz - 1
                far_waits.append(send(part.at[z], other_far.at[dz - 1], ssem.at[k], rsem.at[k], far_peer(dz)))
        for dz in range(1, outer):
            far_waits[dz - 1].wait_recv()
            total = total + other_far[dz - 1]
        full[far, near] = total
        base += outer - 1
        for dz in range(1, outer):
            k = base + dz - 1
            send(full.at[far, near], full.at[far, near], ssem.at[k], rsem.at[k], far_peer(dz))
        spread = base + outer - 1

        def forward(dz):
            for d in range(1, inner):
                k = spread + dz * (inner - 1) + d - 1
                slot = full.at[far_at(-dz), near]
                send(slot, slot, ssem.at[k], rsem.at[k], near_peer(d))

        def take(dz):
            z = far_at(-dz)
            for d in range(1, inner):
                k = spread + dz * (inner - 1) + d - 1
                slot = full.at[z, near_at(-d)]
                remote(slot, slot, ssem.at[k], rsem.at[k], near_peer(d)).wait_recv()
            consume(dz, z, jnp.concatenate([full[z, q] for q in range(inner)], axis=1))

        forward(0)
        for dz in range(1, outer):
            slot = full.at[far_at(-dz), near]
            remote(slot, slot, ssem.at[base + dz - 1], rsem.at[base + dz - 1], far_peer(dz)).wait_recv()
            forward(dz)
            take(dz - 1)
        take(outer - 1)

    form(0, other)
    small[0].wait()
    first_send[...] = left_of(dirs_in[other], other)
    pl.semaphore_wait(barrier, len(greeted))
    first_swap = send(first_send, first_recv, swap_ssem.at[0], swap_rsem.at[0], (me, other))
    matrix_swap = send(inputs.at[other], swapped, swap_ssem.at[1], swap_rsem.at[1], (me, other))
    form(1, core)
    own_left = left_of(dirs_in[core], core)

    small[1].wait()
    gain_cols = gains.shape[2]
    terms = norm_in[0].astype(F32)
    for z in range(outer):
        for q in range(inner):
            p = z * inner + q
            norm_send[q, z] = terms[:, p * gain_cols : (p + 1) * gain_cols]

    first_swap.wait_recv()
    their_left = first_recv[...]
    factor = jnp.concatenate([
        jnp.where(core == 0, own_left, their_left), jnp.where(core == 0, their_left, own_left)
    ], axis=1)

    norm_waits, norm_far_waits = [], []

    def while_summing():
        for d in range(1, inner):
            norm_waits.append(send(norm_send.at[near_at(d)], norm_recv.at[d - 1], norm_ssem.at[d - 1], norm_rsem.at[d - 1], near_peer(d)))
        matrix_swap.wait_recv()

        @pl.loop(0, rows // 16)
        def _(g):
            r = pl.ds(pl.multiple_of(g * 16, 16), 16)
            high[other, r, :], low[other, r, :] = split(swapped[r, :])

    basis = basis_of(left_sum(0, factor, while_summing))

    halves = [jnp.zeros((rank, rows), F32), jnp.zeros((rank, rows), F32)]

    def add_left(dz, z, block):
        for h in range(2):
            halves[h] = halves[h] + left_of(block, h, columns(z))

    right_sum(0, basis, add_left)

    def norm_step():
        total = norm_send[near]
        for d in range(1, inner):
            norm_waits[d - 1].wait_recv()
            total = total + norm_recv[d - 1]
        norm_part[...] = total
        for d in range(1, outer):
            k = inner - 1 + d - 1
            norm_far_waits.append(send(norm_part.at[far_at(d)], norm_far.at[d - 1], norm_ssem.at[k], norm_rsem.at[k], far_peer(d)))

    basis = basis_of(left_sum(1, jnp.concatenate(halves, axis=1), norm_step))
    basis_own[0], basis_own[1] = basis[:, :rows], basis[:, rows:]
    basis_swap = send(basis_own.at[other], basis_other, swap_ssem.at[2], swap_rsem.at[2], (me, other))

    def left_side(half):
        basis_high, basis_low = split(half)
        return jnp.concatenate([basis_high, basis_high, basis_low], axis=0)

    def approx_of(lhs, block):
        dirs_high, dirs_low = split(block)
        return dot_tn(lhs, jnp.concatenate([dirs_high, dirs_low, dirs_high], axis=0)) / replicas

    def finish(m, lhs, z, block):
        new_error[0, m, :, columns(z)] = (inputs[m, :, columns(z)] - approx_of(lhs, block)).astype(BF16)

    dirs_waits = []
    own_side = left_side(basis_own[core])

    def use_own(dz, z, block):
        k = 3 + dz
        dirs_waits.append(send(dirs_all.at[1, z], dirs_other.at[z], swap_ssem.at[k], swap_rsem.at[k], (me, other)))
        finish(core, own_side, z, block)

    right_sum(1, basis, use_own)
    small[2].wait()
    small[3].wait()
    new_weight[core] = weight_in[core] - step_size * approx_of(own_side, dirs_all[1, far, near])
    total = norm_part[far]
    for d in range(1, outer):
        norm_far_waits[d - 1].wait_recv()
        total = total + norm_far[d - 1]
    for m in range(2):
        new_gains[m] = gains_in[m] - step_size * (total[m : m + 1] / replicas)
    basis_swap.wait_recv()
    other_side = left_side(basis_other[...])
    for dz in range(outer):
        z = far_at(-dz)
        dirs_waits[dz].wait_recv()
        finish(other, other_side, z, jnp.concatenate([dirs_other[z, q] for q in range(inner)], axis=1))
    new_weight[other] = weight_in[other] - step_size * approx_of(other_side, dirs_other[far, near])

    for copy in sends:
        copy.wait_send()


def levels(replicas):
    near = max(d for d in range(1, replicas + 1) if replicas % d == 0 and d * d <= replicas)
    return replicas // near, near


def kernel_shards(grad_kv, error_kv, moment_kv, start_dirs, weight_kv, norm_grads, norm_gains):
    outer, inner = levels(lax.axis_size("dp"))
    _, matrices, rows, width = grad_kv.shape
    rank = start_dirs.shape[1]
    gain_cols = norm_gains.shape[2]
    chunks = 2
    hbm, vmem = pl.BlockSpec(memory_space=pltpu.HBM), pl.BlockSpec(memory_space=pltpu.VMEM)
    whole = (matrices, rows, width)
    block = rank // inner
    dma = pltpu.SemaphoreType.DMA
    factor_copies = 2 * (inner - 1) + outer - 1
    dirs_copies = 2 * outer * (inner - 1) + 2 * (outer - 1)
    return pl.pallas_call(
        functools.partial(kernel, outer, inner, chunks),
        out_shape=(
            jax.ShapeDtypeStruct(weight_kv.shape, F32),
            jax.ShapeDtypeStruct(error_kv.shape, BF16),
            jax.ShapeDtypeStruct(moment_kv.shape, BF16),
            jax.ShapeDtypeStruct(norm_gains.shape, F32),
        ),
        in_specs=[hbm] * 7,
        out_specs=(vmem,) * 4,
        scratch_shapes=[
            pltpu.VMEM(whole, BF16), pltpu.VMEM(whole, BF16), pltpu.VMEM(whole, BF16),
            pltpu.VMEM(start_dirs.shape, F32), pltpu.VMEM(weight_kv.shape, F32),
            pltpu.VMEM(norm_grads.shape, BF16), pltpu.VMEM(norm_gains.shape, F32),
            pltpu.VMEM(whole, F32), pltpu.VMEM((rows, width), F32),
            pltpu.VMEM(whole, BF16), pltpu.VMEM(whole, BF16),
            pltpu.VMEM((inner, outer, matrices, gain_cols), F32), pltpu.VMEM((inner - 1, outer, matrices, gain_cols), F32),
            pltpu.VMEM((outer, matrices, gain_cols), F32), pltpu.VMEM((outer - 1, matrices, gain_cols), F32),
            pltpu.VMEM((rank, rows), F32), pltpu.VMEM((rank, rows), F32),
            pltpu.VMEM((2, inner, block, 2 * rows), F32), pltpu.VMEM((2, inner - 1, block, 2 * rows), F32),
            pltpu.VMEM((2, outer, block, 2 * rows), F32), pltpu.VMEM((2, inner, block, 2 * rows), F32),
            pltpu.VMEM((2, outer, inner, rank, LANES), F32), pltpu.VMEM((2, outer, inner - 1, rank, LANES), F32),
            pltpu.VMEM((2, outer, rank, LANES), F32), pltpu.VMEM((2, outer - 1, rank, LANES), F32),
            pltpu.VMEM((2, outer, inner, rank, LANES), F32),
            pltpu.VMEM((2, rank, rows), F32), pltpu.VMEM((rank, rows), F32),
            pltpu.VMEM((outer, inner, rank, LANES), F32),
            dma((6 * chunks + 4,)), dma((3 + outer,)), dma((3 + outer,)),
            dma((inner + outer - 2,)), dma((inner + outer - 2,)),
            dma((2, factor_copies)), dma((2, factor_copies)), dma((2, dirs_copies)), dma((2, dirs_copies)),
        ],
        compiler_params=pltpu.CompilerParams(
            collective_id=0, has_side_effects=True, vmem_limit_bytes=44 * 2**20
        ),
        name="power_step",
    )(grad_kv, error_kv, moment_kv, start_dirs, weight_kv, norm_grads, norm_gains)


def solution(mesh):
    replicas, tensor = mesh.shape["dp"], mesh.shape["tensor"]

    def shards(*args):
        _, matrices, rows, width = args[0].shape
        rank = args[3].shape[1]
        _, near = levels(replicas)
        fits = (
            tensor == matrices == 2
            and near > 1
            and width == LANES * replicas
            and rank % (SUBLANES * near) == 0
            and rows % (2 * LANES) == 0
        )
        return (kernel_shards if fits else plain_shards)(*args)

    return jax.shard_map(
        shards,
        mesh=mesh,
        in_specs=(
            P("dp", None, "tensor", None),
            P("dp", None, "tensor", None),
            P("dp", None, "tensor", None),
            P(),
            P(None, "tensor", "dp"),
            P("dp", None, "tensor"),
            P(None, "tensor", "dp"),
        ),
        out_specs=(
            P(None, "tensor", "dp"),
            P("dp", None, "tensor", None),
            P("dp", None, "tensor", None),
            P(None, "tensor", "dp"),
        ),
        check_vma=False,
    )
```

```python
import functools

import jax
import jax.numpy as jnp
from jax import lax
from jax.experimental import pallas as pl
from jax.experimental.pallas import tpu as pltpu
from jax.sharding import PartitionSpec as P

momentum_decay = 0.9
step_size = 0.5
LANES = 128
SUBLANES = 8
F32 = jnp.float32
BF16 = jnp.bfloat16
HIGHEST = lax.Precision.HIGHEST


def project(inputs, directions):
    return jnp.einsum("mrd,mkd->mrk", inputs, directions, precision=HIGHEST)


def tri_solve(triangle, columns):
    return jax.scipy.linalg.solve_triangular(triangle, columns, lower=True)


def orthonormal(factor):
    full_rows = lax.all_gather(factor, "tensor", axis=1, tiled=True)
    gram_matrix = jnp.einsum("mrk,mrj->mkj", full_rows, full_rows, precision=HIGHEST)
    cholesky_factor = jnp.linalg.cholesky(gram_matrix)
    solved = jax.vmap(tri_solve)(cholesky_factor, jnp.swapaxes(factor, 1, 2))
    return jnp.swapaxes(solved, 1, 2)


def column_sums(inputs, basis):
    partial_sum = jnp.einsum("mrd,mrk->mkd", inputs, basis, precision=HIGHEST)
    return lax.psum(partial_sum, ("dp", "tensor"))


def plain_shards(grad_kv, error_kv, moment_kv, start_dirs, weight_kv, norm_grads, norm_gains):
    replicas = lax.axis_size("dp")
    dp_index = lax.axis_index("dp")
    moment_f = momentum_decay * moment_kv.astype(F32) + grad_kv.astype(F32)
    new_moment_kv = moment_f.astype(BF16)
    inputs = (moment_f + error_kv.astype(F32))[0]
    norm_terms = norm_grads[0].astype(F32)
    gain_cols = norm_gains.shape[2]
    factor = project(inputs, start_dirs)
    factor, norm_total = lax.psum((factor, norm_terms), "dp")
    own_norm = lax.dynamic_slice_in_dim(norm_total, dp_index * gain_cols, gain_cols, 1)
    mean_norm = own_norm / replicas
    basis = orthonormal(factor)
    directions = column_sums(inputs, basis)
    factor = lax.psum(project(inputs, directions), "dp")
    basis = orthonormal(factor)
    directions = column_sums(inputs, basis)
    approx = jnp.einsum("mrk,mkd->mrd", basis, directions, precision=HIGHEST) / replicas
    new_error_kv = (inputs - approx).astype(BF16)[None]
    weight_cols = weight_kv.shape[2]
    own_approx = lax.dynamic_slice_in_dim(approx, dp_index * weight_cols, weight_cols, 2)
    new_weight_kv = weight_kv - step_size * own_approx
    new_gains = norm_gains - step_size * mean_norm[:, None, :]
    return (new_weight_kv, new_error_kv, new_moment_kv, new_gains)


def split(value):
    high = value.astype(BF16)
    return high, (value - high.astype(F32)).astype(BF16)


def dot_nt(a, b):
    return lax.dot_general(a, b, (((1,), (1,)), ((), ())), preferred_element_type=F32)


def dot_tn(a, b):
    return lax.dot_general(a, b, (((0,), (0,)), ((), ())), preferred_element_type=F32)


def basis_of(factor, block=8):
    rank = factor.shape[0]
    gram = lax.dot_general(
        factor, factor, (((1,), (1,)), ((), ())), precision=HIGHEST, preferred_element_type=F32
    )
    row_id = lax.broadcasted_iota(jnp.int32, (rank, 2 * rank), 0)
    col_id = lax.broadcasted_iota(jnp.int32, (rank, 2 * rank), 1)
    unit = (lax.broadcasted_iota(jnp.int32, (rank, rank), 0) == lax.broadcasted_iota(jnp.int32, (rank, rank), 1)).astype(F32)
    work = jnp.concatenate([gram, unit], axis=1)
    for first in range(0, rank, block):
        cols = [jnp.broadcast_to(work[:, j : j + 1], work.shape) for j in range(first, first + block)]
        rows = [work[j : j + 1, :] for j in range(first, first + block)]
        for i in range(block):
            j = first + i
            ratio = jnp.where(row_id > j, cols[i] * (1.0 / cols[i][j : j + 1, :]), 0.0)
            for k in range(i + 1, block):
                cols[k] = cols[k] - ratio * cols[k][j : j + 1, :]
                rows[k] = rows[k] - ratio[first + k : first + k + 1, :] * rows[i]
            work = work - ratio * rows[i]
    pivots = jnp.sum(jnp.where(row_id == col_id, work, 0.0), axis=1, keepdims=True)
    inverse = work[:, rank:] * lax.rsqrt(pivots)
    return jnp.dot(inverse, factor, precision=HIGHEST, preferred_element_type=F32)


def kernel(
    outer, inner, chunks,
    grad, error, moment, start_dirs, norm_grads,
    own_approx, new_error, new_moment, mean_norm,
    grad_in, error_in, moment_in, dirs_in, norm_in, moment_out, error_out, inputs, swapped, high, low,
    norm_send, norm_recv, norm_part, norm_far,
    first_send, first_recv, factor_send, factor_recv, factor_all,
    dirs_send, dirs_near, dirs_part, dirs_far, dirs_all, basis_own, basis_other, dirs_other,
    load_sem, store_sem, swap_ssem, swap_rsem, norm_ssem, norm_rsem, factor_ssem, factor_rsem, dirs_ssem, dirs_rsem,
):
    me, core = lax.axis_index("dp"), lax.axis_index("tensor")
    other = 1 - core
    far, near = lax.div(me, inner), lax.rem(me, inner)
    replicas = outer * inner
    rows, width = inputs.shape[1:]
    rank = dirs_in.shape[1]
    piece_rows = rows // chunks
    span = width // outer
    sends, stores = [], []

    def store(src, dst):
        copy = pltpu.make_async_copy(src, dst, store_sem.at[len(stores)])
        copy.start()
        stores.append(copy)

    def remote(src, dst, send_sem, recv_sem, to):
        return pltpu.make_async_remote_copy(
            src_ref=src, dst_ref=dst, send_sem=send_sem, recv_sem=recv_sem,
            device_id=to, device_id_type=pl.DeviceIdType.MESH,
        )

    def send(*args):
        copy = remote(*args)
        copy.start()
        sends.append(copy)
        return copy

    def near_at(d):
        return lax.rem(near + d + inner, inner)

    def far_at(d):
        return lax.rem(far + d + outer, outer)

    def near_peer(d):
        return (far * inner + near_at(d), core)

    def far_peer(d):
        return (far_at(d) * inner + near, core)

    def peer(d):
        return (lax.rem(me + d + replicas, replicas), core)

    def columns(z):
        return pl.ds(pl.multiple_of(z * span, span), span)

    last = 6 * chunks
    small = [
        pltpu.make_async_copy(src, dst, load_sem.at[last + k])
        for k, (src, dst) in enumerate(((start_dirs, dirs_in), (norm_grads, norm_in)))
    ]
    loads = []
    for i, m in enumerate((other, core)):
        for c in range(chunks):
            r = pl.ds(c * piece_rows, piece_rows)
            loads.append([
                pltpu.make_async_copy(src.at[0, m, r], dst.at[m, r], load_sem.at[(i * chunks + c) * 3 + k])
                for k, (src, dst) in enumerate(((grad, grad_in), (moment, moment_in), (error, error_in)))
            ])
    for n, group in enumerate(loads):
        for copy in group:
            copy.start()
        if n == 0:
            small[0].start()
            small[1].start()

    barrier = pltpu.get_barrier_semaphore()
    greeted = [peer(d) for d in range(1, replicas)] + [(me, other)]
    for device in greeted:
        pl.semaphore_signal(barrier, inc=1, device_id=device, device_id_type=pl.DeviceIdType.MESH)

    def form(i, m):
        for c in range(chunks):
            for copy in loads[i * chunks + c]:
                copy.wait()

            @pl.loop(0, piece_rows // 16)
            def _(g):
                r = pl.ds(pl.multiple_of(c * piece_rows + g * 16, 16), 16)
                moment_f = momentum_decay * moment_in[m, r, :].astype(F32) + grad_in[m, r, :].astype(F32)
                moment_out[m, r, :] = moment_f.astype(BF16)
                x = moment_f + error_in[m, r, :].astype(F32)
                inputs[m, r, :] = x
                high[m, r, :], low[m, r, :] = split(x)

        store(moment_out.at[m], new_moment.at[0, m])

    def left_of(dirs, h, cols=slice(None)):
        dirs_high, dirs_low = split(dirs)
        part = dot_nt(jnp.concatenate([dirs_high, dirs_low], axis=0), high[h, :, cols])
        return part[:rank] + part[rank:] + dot_nt(dirs_high, low[h, :, cols])

    def left_sum(step, factor, between=None):
        own, arrived, full = factor_send.at[step], factor_recv.at[step], factor_all.at[step]
        ssem, rsem = factor_ssem.at[step], factor_rsem.at[step]
        row_blocks = 2 * rows // LANES
        for j in range(replicas):
            a, b = divmod(j, row_blocks)
            own[j] = factor[a * SUBLANES : (a + 1) * SUBLANES, b * LANES : (b + 1) * LANES]
        order = sorted(range(1, replicas), key=lambda d: abs(2 * d - replicas))
        waits = [send(own.at[peer(d)[0]], arrived.at[d - 1], ssem.at[d - 1], rsem.at[d - 1], peer(d)) for d in order]
        if between is not None:
            between()
        for copy in waits:
            copy.wait_recv()
        total = own[me]
        for d in range(1, replicas):
            total = total + arrived[d - 1]
        full[me] = total
        base = replicas - 1
        for d in order:
            send(full.at[me], full.at[me], ssem.at[base + d - 1], rsem.at[base + d - 1], peer(d))
        for d in order:
            slot = full.at[peer(-d)[0]]
            remote(slot, slot, ssem.at[base + d - 1], rsem.at[base + d - 1], peer(d)).wait_recv()
        return jnp.concatenate(
            [
                jnp.concatenate([full[a * row_blocks + b] for b in range(row_blocks)], axis=1)
                for a in range(rank // SUBLANES)
            ],
            axis=0,
        )

    def right_sum(step, basis, consume):
        basis_high, basis_low = split(basis)
        both = jnp.concatenate([basis_high, basis_low], axis=0)
        own, arrived, part, other_far, full = (
            dirs_send.at[step], dirs_near.at[step], dirs_part.at[step], dirs_far.at[step], dirs_all.at[step]
        )
        ssem, rsem = dirs_ssem.at[step], dirs_rsem.at[step]
        order = list(range(1, outer)) + [0]
        waits = {}
        for dz in order:
            z = far_at(dz)
            sums = low_sums = 0.0
            for h in range(2):
                half = slice(h * rows, (h + 1) * rows)
                sums += jnp.dot(both[:, half], high[h, :, columns(z)], preferred_element_type=F32)
                low_sums += jnp.dot(basis_high[:, half], low[h, :, columns(z)], preferred_element_type=F32)
            block = sums[:rank] + sums[rank:] + low_sums
            for q in range(inner):
                own[z, q] = block[:, q * LANES : (q + 1) * LANES]
            for d in range(1, inner):
                k = dz * (inner - 1) + d - 1
                waits[dz, d] = send(own.at[z, near_at(d)], arrived.at[z, d - 1], ssem.at[k], rsem.at[k], near_peer(d))
        base = outer * (inner - 1)
        far_waits = []
        for dz in order:
            z = far_at(dz)
            total = own[z, near]
            for d in range(1, inner):
                waits[dz, d].wait_recv()
                total = total + arrived[z, d - 1]
            if dz:
                part[z] = total
                k = base + dz - 1
                far_waits.append(send(part.at[z], other_far.at[dz - 1], ssem.at[k], rsem.at[k], far_peer(dz)))
        for dz in range(1, outer):
            far_waits[dz - 1].wait_recv()
            total = total + other_far[dz - 1]
        full[far, near] = total
        base += outer - 1
        for dz in range(1, outer):
            k = base + dz - 1
            send(full.at[far, near], full.at[far, near], ssem.at[k], rsem.at[k], far_peer(dz))
        spread = base + outer - 1

        def forward(dz):
            for d in range(1, inner):
                k = spread + dz * (inner - 1) + d - 1
                slot = full.at[far_at(-dz), near]
                send(slot, slot, ssem.at[k], rsem.at[k], near_peer(d))

        def take(dz):
            z = far_at(-dz)
            for d in range(1, inner):
                k = spread + dz * (inner - 1) + d - 1
                slot = full.at[z, near_at(-d)]
                remote(slot, slot, ssem.at[k], rsem.at[k], near_peer(d)).wait_recv()
            consume(dz, z, jnp.concatenate([full[z, q] for q in range(inner)], axis=1))

        forward(0)
        for dz in range(1, outer):
            slot = full.at[far_at(-dz), near]
            remote(slot, slot, ssem.at[base + dz - 1], rsem.at[base + dz - 1], far_peer(dz)).wait_recv()
            forward(dz)
            take(dz - 1)
        take(outer - 1)

    form(0, other)
    small[0].wait()
    first_send[...] = left_of(dirs_in[other], other)
    pl.semaphore_wait(barrier, len(greeted))
    first_swap = send(first_send, first_recv, swap_ssem.at[0], swap_rsem.at[0], (me, other))
    matrix_swap = send(inputs.at[other], swapped, swap_ssem.at[1], swap_rsem.at[1], (me, other))
    form(1, core)
    own_left = left_of(dirs_in[core], core)

    small[1].wait()
    gain_cols = mean_norm.shape[2]
    terms = norm_in[0].astype(F32)
    for z in range(outer):
        for q in range(inner):
            p = z * inner + q
            norm_send[q, z] = terms[:, p * gain_cols : (p + 1) * gain_cols]

    first_swap.wait_recv()
    their_left = first_recv[...]
    factor = jnp.concatenate([
        jnp.where(core == 0, own_left, their_left), jnp.where(core == 0, their_left, own_left)
    ], axis=1)

    norm_waits, norm_far_waits = [], []

    def while_summing():
        for d in range(1, inner):
            norm_waits.append(send(norm_send.at[near_at(d)], norm_recv.at[d - 1], norm_ssem.at[d - 1], norm_rsem.at[d - 1], near_peer(d)))
        matrix_swap.wait_recv()

        @pl.loop(0, rows // 16)
        def _(g):
            r = pl.ds(pl.multiple_of(g * 16, 16), 16)
            high[other, r, :], low[other, r, :] = split(swapped[r, :])

    basis = basis_of(left_sum(0, factor, while_summing))

    halves = [jnp.zeros((rank, rows), F32), jnp.zeros((rank, rows), F32)]

    def add_left(dz, z, block):
        for h in range(2):
            halves[h] = halves[h] + left_of(block, h, columns(z))

    right_sum(0, basis, add_left)

    def norm_step():
        total = norm_send[near]
        for d in range(1, inner):
            norm_waits[d - 1].wait_recv()
            total = total + norm_recv[d - 1]
        norm_part[...] = total
        for d in range(1, outer):
            k = inner - 1 + d - 1
            norm_far_waits.append(send(norm_part.at[far_at(d)], norm_far.at[d - 1], norm_ssem.at[k], norm_rsem.at[k], far_peer(d)))

    basis = basis_of(left_sum(1, jnp.concatenate(halves, axis=1), norm_step))
    basis_own[0], basis_own[1] = basis[:, :rows], basis[:, rows:]
    basis_swap = send(basis_own.at[other], basis_other, swap_ssem.at[2], swap_rsem.at[2], (me, other))

    def left_side(half):
        basis_high, basis_low = split(half)
        return jnp.concatenate([basis_high, basis_high, basis_low], axis=0)

    def approx_of(lhs, block):
        dirs_high, dirs_low = split(block)
        return dot_tn(lhs, jnp.concatenate([dirs_high, dirs_low, dirs_high], axis=0)) / replicas

    def finish(m, lhs, z, block):
        error_out[m, :, columns(z)] = (inputs[m, :, columns(z)] - approx_of(lhs, block)).astype(BF16)
        store(error_out.at[m, :, columns(z)], new_error.at[0, m, :, columns(z)])

    dirs_waits = []
    own_side = left_side(basis_own[core])

    def use_own(dz, z, block):
        k = 3 + dz
        dirs_waits.append(send(dirs_all.at[1, z], dirs_other.at[z], swap_ssem.at[k], swap_rsem.at[k], (me, other)))
        finish(core, own_side, z, block)

    right_sum(1, basis, use_own)
    own_approx[core] = approx_of(own_side, dirs_all[1, far, near])
    total = norm_part[far]
    for d in range(1, outer):
        norm_far_waits[d - 1].wait_recv()
        total = total + norm_far[d - 1]
    for m in range(2):
        mean_norm[m] = total[m : m + 1] / replicas
    basis_swap.wait_recv()
    other_side = left_side(basis_other[...])
    for dz in range(outer):
        z = far_at(-dz)
        dirs_waits[dz].wait_recv()
        finish(other, other_side, z, jnp.concatenate([dirs_other[z, q] for q in range(inner)], axis=1))
    own_approx[other] = approx_of(other_side, dirs_other[far, near])

    for copy in sends:
        copy.wait_send()
    for copy in stores:
        copy.wait()


def levels(replicas):
    near = max(d for d in range(1, replicas + 1) if replicas % d == 0 and d * d <= replicas)
    return replicas // near, near


def kernel_shards(grad_kv, error_kv, moment_kv, start_dirs, weight_kv, norm_grads, norm_gains):
    outer, inner = levels(lax.axis_size("dp"))
    _, matrices, rows, width = grad_kv.shape
    rank = start_dirs.shape[1]
    gain_cols = norm_gains.shape[2]
    chunks = 2
    hbm, vmem = pl.BlockSpec(memory_space=pltpu.HBM), pl.BlockSpec(memory_space=pltpu.VMEM)
    whole = (matrices, rows, width)
    dma = pltpu.SemaphoreType.DMA
    replicas = outer * inner
    factor_copies = 2 * (replicas - 1)
    tile = (SUBLANES, LANES)
    dirs_copies = 2 * outer * (inner - 1) + 2 * (outer - 1)
    own_approx, new_error_kv, new_moment_kv, mean_norm = pl.pallas_call(
        functools.partial(kernel, outer, inner, chunks),
        out_shape=(
            jax.ShapeDtypeStruct(weight_kv.shape, F32),
            jax.ShapeDtypeStruct(error_kv.shape, BF16),
            jax.ShapeDtypeStruct(moment_kv.shape, BF16),
            jax.ShapeDtypeStruct(norm_gains.shape, F32),
        ),
        in_specs=[hbm] * 5,
        out_specs=(vmem, hbm, hbm, vmem),
        scratch_shapes=[
            pltpu.VMEM(whole, BF16), pltpu.VMEM(whole, BF16), pltpu.VMEM(whole, BF16),
            pltpu.VMEM(start_dirs.shape, F32), pltpu.VMEM(norm_grads.shape, BF16),
            pltpu.VMEM(whole, BF16), pltpu.VMEM(whole, BF16),
            pltpu.VMEM(whole, F32), pltpu.VMEM((rows, width), F32),
            pltpu.VMEM(whole, BF16), pltpu.VMEM(whole, BF16),
            pltpu.VMEM((inner, outer, matrices, gain_cols), F32), pltpu.VMEM((inner - 1, outer, matrices, gain_cols), F32),
            pltpu.VMEM((outer, matrices, gain_cols), F32), pltpu.VMEM((outer - 1, matrices, gain_cols), F32),
            pltpu.VMEM((rank, rows), F32), pltpu.VMEM((rank, rows), F32),
            pltpu.VMEM((2, replicas) + tile, F32), pltpu.VMEM((2, replicas - 1) + tile, F32),
            pltpu.VMEM((2, replicas) + tile, F32),
            pltpu.VMEM((2, outer, inner, rank, LANES), F32), pltpu.VMEM((2, outer, inner - 1, rank, LANES), F32),
            pltpu.VMEM((2, outer, rank, LANES), F32), pltpu.VMEM((2, outer - 1, rank, LANES), F32),
            pltpu.VMEM((2, outer, inner, rank, LANES), F32),
            pltpu.VMEM((2, rank, rows), F32), pltpu.VMEM((rank, rows), F32),
            pltpu.VMEM((outer, inner, rank, LANES), F32),
            dma((6 * chunks + 2,)), dma((2 + 2 * outer,)), dma((3 + outer,)), dma((3 + outer,)),
            dma((inner + outer - 2,)), dma((inner + outer - 2,)),
            dma((2, factor_copies)), dma((2, factor_copies)), dma((2, dirs_copies)), dma((2, dirs_copies)),
        ],
        compiler_params=pltpu.CompilerParams(
            collective_id=0, has_side_effects=True, vmem_limit_bytes=62 * 2**20
        ),
        name="power_step",
    )(grad_kv, error_kv, moment_kv, start_dirs, norm_grads)
    new_weight_kv = weight_kv - step_size * own_approx
    new_gains = norm_gains - step_size * mean_norm
    return (new_weight_kv, new_error_kv, new_moment_kv, new_gains)


def solution(mesh):
    replicas, tensor = mesh.shape["dp"], mesh.shape["tensor"]

    def shards(*args):
        _, matrices, rows, width = args[0].shape
        rank = args[3].shape[1]
        _, near = levels(replicas)
        fits = (
            tensor == matrices == 2
            and near > 1
            and width == LANES * replicas
            and (rank // SUBLANES) * (2 * rows // LANES) == replicas
            and rank % SUBLANES == 0
            and rows % (2 * LANES) == 0
        )
        return (kernel_shards if fits else plain_shards)(*args)

    return jax.shard_map(
        shards,
        mesh=mesh,
        in_specs=(
            P("dp", None, "tensor", None),
            P("dp", None, "tensor", None),
            P("dp", None, "tensor", None),
            P(),
            P(None, "tensor", "dp"),
            P("dp", None, "tensor"),
            P(None, "tensor", "dp"),
        ),
        out_specs=(
            P(None, "tensor", "dp"),
            P("dp", None, "tensor", None),
            P("dp", None, "tensor", None),
            P(None, "tensor", "dp"),
        ),
        check_vma=False,
    )
```

```python
import functools

import jax
import jax.numpy as jnp
from jax import lax
from jax.experimental import pallas as pl
from jax.experimental.pallas import tpu as pltpu
from jax.sharding import PartitionSpec as P

momentum_decay = 0.9
step_size = 0.5
LANES = 128
SUBLANES = 8
F32 = jnp.float32
BF16 = jnp.bfloat16
HIGHEST = lax.Precision.HIGHEST


def project(inputs, directions):
    return jnp.einsum("mrd,mkd->mrk", inputs, directions, precision=HIGHEST)


def tri_solve(triangle, columns):
    return jax.scipy.linalg.solve_triangular(triangle, columns, lower=True)


def orthonormal(factor):
    full_rows = lax.all_gather(factor, "tensor", axis=1, tiled=True)
    gram_matrix = jnp.einsum("mrk,mrj->mkj", full_rows, full_rows, precision=HIGHEST)
    cholesky_factor = jnp.linalg.cholesky(gram_matrix)
    solved = jax.vmap(tri_solve)(cholesky_factor, jnp.swapaxes(factor, 1, 2))
    return jnp.swapaxes(solved, 1, 2)


def column_sums(inputs, basis):
    partial_sum = jnp.einsum("mrd,mrk->mkd", inputs, basis, precision=HIGHEST)
    return lax.psum(partial_sum, ("dp", "tensor"))


def plain_shards(grad_kv, error_kv, moment_kv, start_dirs, weight_kv, norm_grads, norm_gains):
    replicas = lax.axis_size("dp")
    dp_index = lax.axis_index("dp")
    moment_f = momentum_decay * moment_kv.astype(F32) + grad_kv.astype(F32)
    new_moment_kv = moment_f.astype(BF16)
    inputs = (moment_f + error_kv.astype(F32))[0]
    norm_terms = norm_grads[0].astype(F32)
    gain_cols = norm_gains.shape[2]
    factor = project(inputs, start_dirs)
    factor, norm_total = lax.psum((factor, norm_terms), "dp")
    own_norm = lax.dynamic_slice_in_dim(norm_total, dp_index * gain_cols, gain_cols, 1)
    mean_norm = own_norm / replicas
    basis = orthonormal(factor)
    directions = column_sums(inputs, basis)
    factor = lax.psum(project(inputs, directions), "dp")
    basis = orthonormal(factor)
    directions = column_sums(inputs, basis)
    approx = jnp.einsum("mrk,mkd->mrd", basis, directions, precision=HIGHEST) / replicas
    new_error_kv = (inputs - approx).astype(BF16)[None]
    weight_cols = weight_kv.shape[2]
    own_approx = lax.dynamic_slice_in_dim(approx, dp_index * weight_cols, weight_cols, 2)
    new_weight_kv = weight_kv - step_size * own_approx
    new_gains = norm_gains - step_size * mean_norm[:, None, :]
    return (new_weight_kv, new_error_kv, new_moment_kv, new_gains)


def split(value):
    high = value.astype(BF16)
    return high, (value - high.astype(F32)).astype(BF16)


def dot_nt(a, b):
    return lax.dot_general(a, b, (((1,), (1,)), ((), ())), preferred_element_type=F32)


def basis_of(factor, table, block=4):
    rank = factor.shape[0]
    gram = lax.dot_general(
        factor, factor, (((1,), (1,)), ((), ())), precision=HIGHEST, preferred_element_type=F32
    )
    shape = (SUBLANES, LANES)
    lane = lax.broadcasted_iota(jnp.int32, (rank, LANES), 1)
    line = lax.broadcasted_iota(jnp.int32, (rank, LANES), 0)
    table[...] = jnp.concatenate([gram, (lane == line + rank).astype(F32)[:, rank:]], axis=1)
    rows = [jnp.broadcast_to(table[i : i + 1, :], shape) for i in range(rank)]
    for first in range(0, rank, block):
        cols = [
            {i: jnp.broadcast_to(rows[i][:, j : j + 1], shape) for i in range(first, rank)}
            for j in range(first, first + block)
        ]
        for n in range(block):
            j = first + n
            pivot = cols[n][j]
            inverse = 1.0 / pivot
            for i in range(j + 1, rank):
                ratio = cols[n][i] * inverse
                for k in range(n + 1, block):
                    cols[k][i] = cols[k][i] - ratio * cols[k][j]
                rows[i] = rows[i] - ratio * rows[j]
            table[j : j + 1, :] = (rows[j] * lax.rsqrt(pivot))[:1]
    return jnp.dot(table[:, rank : 2 * rank], factor, precision=HIGHEST, preferred_element_type=F32)


def kernel(
    outer, inner, chunks,
    grad, error, moment, start_dirs, norm_grads,
    own_approx, new_error, new_moment, mean_norm,
    grad_in, error_in, moment_in, dirs_in, norm_in, moment_out, error_out, inputs, swapped, high, low,
    norm_send, norm_recv, norm_part, norm_far,
    first_send, first_recv, factor_send, factor_recv, factor_all,
    dirs_send, dirs_near, dirs_part, dirs_far, dirs_all, basis_own, basis_other, dirs_other, table,
    load_sem, store_sem, swap_ssem, swap_rsem, norm_ssem, norm_rsem, factor_ssem, factor_rsem, dirs_ssem, dirs_rsem,
):
    me, core = lax.axis_index("dp"), lax.axis_index("tensor")
    other = 1 - core
    far, near = lax.div(me, inner), lax.rem(me, inner)
    replicas = outer * inner
    rows, width = inputs.shape[1:]
    rank = dirs_in.shape[1]
    piece_rows = rows // chunks
    span = width // outer
    sends, stores = [], []

    def store(src, dst):
        copy = pltpu.make_async_copy(src, dst, store_sem.at[len(stores)])
        copy.start()
        stores.append(copy)

    def remote(src, dst, send_sem, recv_sem, to):
        return pltpu.make_async_remote_copy(
            src_ref=src, dst_ref=dst, send_sem=send_sem, recv_sem=recv_sem,
            device_id=to, device_id_type=pl.DeviceIdType.MESH,
        )

    def send(*args):
        copy = remote(*args)
        copy.start()
        sends.append(copy)
        return copy

    def near_at(d):
        return lax.rem(near + d + inner, inner)

    def far_at(d):
        return lax.rem(far + d + outer, outer)

    def near_peer(d):
        return (far * inner + near_at(d), core)

    def far_peer(d):
        return (far_at(d) * inner + near, core)

    def peer(d):
        return (lax.rem(me + d + replicas, replicas), core)

    def columns(z):
        return pl.ds(pl.multiple_of(z * span, span), span)

    last = 6 * chunks
    small = [
        pltpu.make_async_copy(src, dst, load_sem.at[last + k])
        for k, (src, dst) in enumerate(((start_dirs, dirs_in), (norm_grads, norm_in)))
    ]
    loads = []
    for i, m in enumerate((other, core)):
        for c in range(chunks):
            r = pl.ds(c * piece_rows, piece_rows)
            loads.append([
                pltpu.make_async_copy(src.at[0, m, r], dst.at[m, r], load_sem.at[(i * chunks + c) * 3 + k])
                for k, (src, dst) in enumerate(((grad, grad_in), (moment, moment_in), (error, error_in)))
            ])
    for n, group in enumerate(loads):
        for copy in group:
            copy.start()
        if n == 0:
            small[0].start()
            small[1].start()

    barrier = pltpu.get_barrier_semaphore()
    greeted = [peer(d) for d in range(1, replicas)] + [(me, other)]
    for device in greeted:
        pl.semaphore_signal(barrier, inc=1, device_id=device, device_id_type=pl.DeviceIdType.MESH)

    def form(i, m):
        for c in range(chunks):
            for copy in loads[i * chunks + c]:
                copy.wait()

            @pl.loop(0, piece_rows // 16)
            def _(g):
                r = pl.ds(pl.multiple_of(c * piece_rows + g * 16, 16), 16)
                moment_f = momentum_decay * moment_in[m, r, :].astype(F32) + grad_in[m, r, :].astype(F32)
                moment_out[m, r, :] = moment_f.astype(BF16)
                x = moment_f + error_in[m, r, :].astype(F32)
                inputs[m, r, :] = x
                high[m, r, :], low[m, r, :] = split(x)

        store(moment_out.at[m], new_moment.at[0, m])

    def left_of(dirs, h, cols=slice(None)):
        dirs_high, dirs_low = split(dirs)
        both = jnp.concatenate([dirs_high, dirs_low], axis=0)
        return dot_nt(high[h, :, cols], both), dot_nt(low[h, :, cols], dirs_high)

    def joined(wide, narrow):
        turned = wide.T
        return turned[:rank] + turned[rank:] + narrow.T

    def left_sum(step, factor, between=None):
        own, arrived, full = factor_send.at[step], factor_recv.at[step], factor_all.at[step]
        ssem, rsem = factor_ssem.at[step], factor_rsem.at[step]
        row_blocks = 2 * rows // LANES
        for j in range(replicas):
            a, b = divmod(j, row_blocks)
            own[j] = factor[a * SUBLANES : (a + 1) * SUBLANES, b * LANES : (b + 1) * LANES]
        order = sorted(range(1, replicas), key=lambda d: abs(2 * d - replicas))
        waits = [send(own.at[peer(d)[0]], arrived.at[d - 1], ssem.at[d - 1], rsem.at[d - 1], peer(d)) for d in order]
        if between is not None:
            between()
        for copy in waits:
            copy.wait_recv()
        total = own[me]
        for d in range(1, replicas):
            total = total + arrived[d - 1]
        full[me] = total
        base = replicas - 1
        for d in order:
            send(full.at[me], full.at[me], ssem.at[base + d - 1], rsem.at[base + d - 1], peer(d))
        for d in order:
            slot = full.at[peer(-d)[0]]
            remote(slot, slot, ssem.at[base + d - 1], rsem.at[base + d - 1], peer(d)).wait_recv()
        return jnp.concatenate(
            [
                jnp.concatenate([full[a * row_blocks + b] for b in range(row_blocks)], axis=1)
                for a in range(rank // SUBLANES)
            ],
            axis=0,
        )

    def right_sum(step, basis, consume):
        basis_high, basis_low = split(basis)
        both = jnp.concatenate([basis_high, basis_low], axis=0)
        own, arrived, part, other_far, full = (
            dirs_send.at[step], dirs_near.at[step], dirs_part.at[step], dirs_far.at[step], dirs_all.at[step]
        )
        ssem, rsem = dirs_ssem.at[step], dirs_rsem.at[step]
        order = list(range(1, outer)) + [0]
        waits = {}
        for dz in order:
            z = far_at(dz)
            sums = low_sums = 0.0
            for h in range(2):
                half = slice(h * rows, (h + 1) * rows)
                sums += jnp.dot(both[:, half], high[h, :, columns(z)], preferred_element_type=F32)
                low_sums += jnp.dot(basis_high[:, half], low[h, :, columns(z)], preferred_element_type=F32)
            block = sums[:rank] + sums[rank:] + low_sums
            for q in range(inner):
                own[z, q] = block[:, q * LANES : (q + 1) * LANES]
            for d in range(1, inner):
                k = dz * (inner - 1) + d - 1
                waits[dz, d] = send(own.at[z, near_at(d)], arrived.at[z, d - 1], ssem.at[k], rsem.at[k], near_peer(d))
        base = outer * (inner - 1)
        far_waits = []
        for dz in order:
            z = far_at(dz)
            total = own[z, near]
            for d in range(1, inner):
                waits[dz, d].wait_recv()
                total = total + arrived[z, d - 1]
            if dz:
                part[z] = total
                k = base + dz - 1
                far_waits.append(send(part.at[z], other_far.at[dz - 1], ssem.at[k], rsem.at[k], far_peer(dz)))
        for dz in range(1, outer):
            far_waits[dz - 1].wait_recv()
            total = total + other_far[dz - 1]
        full[far, near] = total
        base += outer - 1
        for dz in range(1, outer):
            k = base + dz - 1
            send(full.at[far, near], full.at[far, near], ssem.at[k], rsem.at[k], far_peer(dz))
        spread = base + outer - 1

        def forward(dz):
            for d in range(1, inner):
                k = spread + dz * (inner - 1) + d - 1
                slot = full.at[far_at(-dz), near]
                send(slot, slot, ssem.at[k], rsem.at[k], near_peer(d))

        def take(dz):
            z = far_at(-dz)
            for d in range(1, inner):
                k = spread + dz * (inner - 1) + d - 1
                slot = full.at[z, near_at(-d)]
                remote(slot, slot, ssem.at[k], rsem.at[k], near_peer(d)).wait_recv()
            consume(dz, z, jnp.concatenate([full[z, q] for q in range(inner)], axis=1))

        forward(0)
        for dz in range(1, outer):
            slot = full.at[far_at(-dz), near]
            remote(slot, slot, ssem.at[base + dz - 1], rsem.at[base + dz - 1], far_peer(dz)).wait_recv()
            forward(dz)
            take(dz - 1)
        take(outer - 1)

    form(0, other)
    small[0].wait()
    first_send[...] = joined(*left_of(dirs_in[other], other))
    pl.semaphore_wait(barrier, len(greeted))
    first_swap = send(first_send, first_recv, swap_ssem.at[0], swap_rsem.at[0], (me, other))
    matrix_swap = send(inputs.at[other], swapped, swap_ssem.at[1], swap_rsem.at[1], (me, other))
    form(1, core)
    own_left = joined(*left_of(dirs_in[core], core))

    small[1].wait()
    gain_cols = mean_norm.shape[2]
    terms = norm_in[0].astype(F32)
    for z in range(outer):
        for q in range(inner):
            p = z * inner + q
            norm_send[q, z] = terms[:, p * gain_cols : (p + 1) * gain_cols]

    first_swap.wait_recv()
    their_left = first_recv[...]
    factor = jnp.concatenate([
        jnp.where(core == 0, own_left, their_left), jnp.where(core == 0, their_left, own_left)
    ], axis=1)

    norm_waits, norm_far_waits = [], []

    def while_summing():
        for d in range(1, inner):
            norm_waits.append(send(norm_send.at[near_at(d)], norm_recv.at[d - 1], norm_ssem.at[d - 1], norm_rsem.at[d - 1], near_peer(d)))
        matrix_swap.wait_recv()

        @pl.loop(0, rows // 16)
        def _(g):
            r = pl.ds(pl.multiple_of(g * 16, 16), 16)
            high[other, r, :], low[other, r, :] = split(swapped[r, :])

    basis = basis_of(left_sum(0, factor, while_summing), table)

    halves = [(0.0, 0.0), (0.0, 0.0)]

    def add_left(dz, z, block):
        for h in range(2):
            wide, narrow = left_of(block, h, columns(z))
            halves[h] = (halves[h][0] + wide, halves[h][1] + narrow)

    right_sum(0, basis, add_left)

    def norm_step():
        total = norm_send[near]
        for d in range(1, inner):
            norm_waits[d - 1].wait_recv()
            total = total + norm_recv[d - 1]
        norm_part[...] = total
        for d in range(1, outer):
            k = inner - 1 + d - 1
            norm_far_waits.append(send(norm_part.at[far_at(d)], norm_far.at[d - 1], norm_ssem.at[k], norm_rsem.at[k], far_peer(d)))

    basis = basis_of(left_sum(1, jnp.concatenate([joined(*half) for half in halves], axis=1), norm_step), table)
    basis_own[0], basis_own[1] = basis[:, :rows], basis[:, rows:]
    basis_swap = send(basis_own.at[other], basis_other, swap_ssem.at[2], swap_rsem.at[2], (me, other))

    def left_side(half):
        basis_high, basis_low = split(half)
        return jnp.concatenate([basis_high, basis_high, basis_low], axis=0).astype(F32).T.astype(BF16)

    def approx_of(lhs, block):
        dirs_high, dirs_low = split(block)
        rhs = jnp.concatenate([dirs_high, dirs_low, dirs_high], axis=0)
        return jnp.dot(lhs, rhs, preferred_element_type=F32) / replicas

    def finish(m, lhs, z, block):
        error_out[m, :, columns(z)] = (inputs[m, :, columns(z)] - approx_of(lhs, block)).astype(BF16)
        store(error_out.at[m, :, columns(z)], new_error.at[0, m, :, columns(z)])

    dirs_waits = []
    own_side = left_side(basis_own[core])

    def use_own(dz, z, block):
        k = 3 + dz
        dirs_waits.append(send(dirs_all.at[1, z], dirs_other.at[z], swap_ssem.at[k], swap_rsem.at[k], (me, other)))
        finish(core, own_side, z, block)

    right_sum(1, basis, use_own)
    own_approx[core] = approx_of(own_side, dirs_all[1, far, near])
    total = norm_part[far]
    for d in range(1, outer):
        norm_far_waits[d - 1].wait_recv()
        total = total + norm_far[d - 1]
    for m in range(2):
        mean_norm[m] = total[m : m + 1] / replicas
    basis_swap.wait_recv()
    other_side = left_side(basis_other[...])
    for dz in range(outer):
        z = far_at(-dz)
        dirs_waits[dz].wait_recv()
        finish(other, other_side, z, jnp.concatenate([dirs_other[z, q] for q in range(inner)], axis=1))
    own_approx[other] = approx_of(other_side, dirs_other[far, near])

    for copy in sends:
        copy.wait_send()
    for copy in stores:
        copy.wait()


def levels(replicas):
    near = max(d for d in range(1, replicas + 1) if replicas % d == 0 and d * d <= replicas)
    return replicas // near, near


def kernel_shards(grad_kv, error_kv, moment_kv, start_dirs, weight_kv, norm_grads, norm_gains):
    outer, inner = levels(lax.axis_size("dp"))
    _, matrices, rows, width = grad_kv.shape
    rank = start_dirs.shape[1]
    gain_cols = norm_gains.shape[2]
    chunks = 2
    hbm, vmem = pl.BlockSpec(memory_space=pltpu.HBM), pl.BlockSpec(memory_space=pltpu.VMEM)
    whole = (matrices, rows, width)
    dma = pltpu.SemaphoreType.DMA
    replicas = outer * inner
    factor_copies = 2 * (replicas - 1)
    tile = (SUBLANES, LANES)
    dirs_copies = 2 * outer * (inner - 1) + 2 * (outer - 1)
    own_approx, new_error_kv, new_moment_kv, mean_norm = pl.pallas_call(
        functools.partial(kernel, outer, inner, chunks),
        out_shape=(
            jax.ShapeDtypeStruct(weight_kv.shape, F32),
            jax.ShapeDtypeStruct(error_kv.shape, BF16),
            jax.ShapeDtypeStruct(moment_kv.shape, BF16),
            jax.ShapeDtypeStruct(norm_gains.shape, F32),
        ),
        in_specs=[hbm] * 5,
        out_specs=(vmem, hbm, hbm, vmem),
        scratch_shapes=[
            pltpu.VMEM(whole, BF16), pltpu.VMEM(whole, BF16), pltpu.VMEM(whole, BF16),
            pltpu.VMEM(start_dirs.shape, F32), pltpu.VMEM(norm_grads.shape, BF16),
            pltpu.VMEM(whole, BF16), pltpu.VMEM(whole, BF16),
            pltpu.VMEM(whole, F32), pltpu.VMEM((rows, width), F32),
            pltpu.VMEM(whole, BF16), pltpu.VMEM(whole, BF16),
            pltpu.VMEM((inner, outer, matrices, gain_cols), F32), pltpu.VMEM((inner - 1, outer, matrices, gain_cols), F32),
            pltpu.VMEM((outer, matrices, gain_cols), F32), pltpu.VMEM((outer - 1, matrices, gain_cols), F32),
            pltpu.VMEM((rank, rows), F32), pltpu.VMEM((rank, rows), F32),
            pltpu.VMEM((2, replicas) + tile, F32), pltpu.VMEM((2, replicas - 1) + tile, F32),
            pltpu.VMEM((2, replicas) + tile, F32),
            pltpu.VMEM((2, outer, inner, rank, LANES), F32), pltpu.VMEM((2, outer, inner - 1, rank, LANES), F32),
            pltpu.VMEM((2, outer, rank, LANES), F32), pltpu.VMEM((2, outer - 1, rank, LANES), F32),
            pltpu.VMEM((2, outer, inner, rank, LANES), F32),
            pltpu.VMEM((2, rank, rows), F32), pltpu.VMEM((rank, rows), F32),
            pltpu.VMEM((outer, inner, rank, LANES), F32), pltpu.VMEM((rank, LANES), F32),
            dma((6 * chunks + 2,)), dma((2 + 2 * outer,)), dma((3 + outer,)), dma((3 + outer,)),
            dma((inner + outer - 2,)), dma((inner + outer - 2,)),
            dma((2, factor_copies)), dma((2, factor_copies)), dma((2, dirs_copies)), dma((2, dirs_copies)),
        ],
        compiler_params=pltpu.CompilerParams(
            collective_id=0, has_side_effects=True, vmem_limit_bytes=48 * 2**20
        ),
        name="power_step",
    )(grad_kv, error_kv, moment_kv, start_dirs, norm_grads)
    new_weight_kv = weight_kv - step_size * own_approx
    new_gains = norm_gains - step_size * mean_norm
    return (new_weight_kv, new_error_kv, new_moment_kv, new_gains)


def solution(mesh):
    replicas, tensor = mesh.shape["dp"], mesh.shape["tensor"]

    def shards(*args):
        _, matrices, rows, width = args[0].shape
        rank = args[3].shape[1]
        _, near = levels(replicas)
        fits = (
            tensor == matrices == 2
            and near > 1
            and width == LANES * replicas
            and (rank // SUBLANES) * (2 * rows // LANES) == replicas
            and rank % SUBLANES == 0
            and rows % (2 * LANES) == 0
        )
        return (kernel_shards if fits else plain_shards)(*args)

    return jax.shard_map(
        shards,
        mesh=mesh,
        in_specs=(
            P("dp", None, "tensor", None),
            P("dp", None, "tensor", None),
            P("dp", None, "tensor", None),
            P(),
            P(None, "tensor", "dp"),
            P("dp", None, "tensor"),
            P(None, "tensor", "dp"),
        ),
        out_specs=(
            P(None, "tensor", "dp"),
            P("dp", None, "tensor", None),
            P("dp", None, "tensor", None),
            P(None, "tensor", "dp"),
        ),
        check_vma=False,
    )
```

```python
import functools

import jax
import jax.numpy as jnp
from jax import lax
from jax.experimental import pallas as pl
from jax.experimental.pallas import tpu as pltpu
from jax.sharding import PartitionSpec as P

momentum_decay = 0.9
step_size = 0.5
LANES = 128
SUBLANES = 8
F32 = jnp.float32
BF16 = jnp.bfloat16
HIGHEST = lax.Precision.HIGHEST


def project(inputs, directions):
    return jnp.einsum("mrd,mkd->mrk", inputs, directions, precision=HIGHEST)


def tri_solve(triangle, columns):
    return jax.scipy.linalg.solve_triangular(triangle, columns, lower=True)


def orthonormal(factor):
    full_rows = lax.all_gather(factor, "tensor", axis=1, tiled=True)
    gram_matrix = jnp.einsum("mrk,mrj->mkj", full_rows, full_rows, precision=HIGHEST)
    cholesky_factor = jnp.linalg.cholesky(gram_matrix)
    solved = jax.vmap(tri_solve)(cholesky_factor, jnp.swapaxes(factor, 1, 2))
    return jnp.swapaxes(solved, 1, 2)


def column_sums(inputs, basis):
    partial_sum = jnp.einsum("mrd,mrk->mkd", inputs, basis, precision=HIGHEST)
    return lax.psum(partial_sum, ("dp", "tensor"))


def plain_shards(grad_kv, error_kv, moment_kv, start_dirs, weight_kv, norm_grads, norm_gains):
    replicas = lax.axis_size("dp")
    dp_index = lax.axis_index("dp")
    moment_f = momentum_decay * moment_kv.astype(F32) + grad_kv.astype(F32)
    new_moment_kv = moment_f.astype(BF16)
    inputs = (moment_f + error_kv.astype(F32))[0]
    norm_terms = norm_grads[0].astype(F32)
    gain_cols = norm_gains.shape[2]
    factor = project(inputs, start_dirs)
    factor, norm_total = lax.psum((factor, norm_terms), "dp")
    own_norm = lax.dynamic_slice_in_dim(norm_total, dp_index * gain_cols, gain_cols, 1)
    mean_norm = own_norm / replicas
    basis = orthonormal(factor)
    directions = column_sums(inputs, basis)
    factor = lax.psum(project(inputs, directions), "dp")
    basis = orthonormal(factor)
    directions = column_sums(inputs, basis)
    approx = jnp.einsum("mrk,mkd->mrd", basis, directions, precision=HIGHEST) / replicas
    new_error_kv = (inputs - approx).astype(BF16)[None]
    weight_cols = weight_kv.shape[2]
    own_approx = lax.dynamic_slice_in_dim(approx, dp_index * weight_cols, weight_cols, 2)
    new_weight_kv = weight_kv - step_size * own_approx
    new_gains = norm_gains - step_size * mean_norm[:, None, :]
    return (new_weight_kv, new_error_kv, new_moment_kv, new_gains)


def split(value):
    high = value.astype(BF16)
    return high, (value - high.astype(F32)).astype(BF16)


def dot_nt(a, b):
    return lax.dot_general(a, b, (((1,), (1,)), ((), ())), preferred_element_type=F32)


def basis_of(factor, table, block=4):
    rank = factor.shape[0]
    gram = lax.dot_general(
        factor, factor, (((1,), (1,)), ((), ())), precision=HIGHEST, preferred_element_type=F32
    )
    shape = (SUBLANES, LANES)
    lane = lax.broadcasted_iota(jnp.int32, (rank, LANES), 1)
    line = lax.broadcasted_iota(jnp.int32, (rank, LANES), 0)
    table[...] = jnp.concatenate([gram, (lane == line + rank).astype(F32)[:, rank:]], axis=1)
    rows = [jnp.broadcast_to(table[i : i + 1, :], shape) for i in range(rank)]
    for first in range(0, rank, block):
        cols = [
            {i: jnp.broadcast_to(rows[i][:, j : j + 1], shape) for i in range(first, rank)}
            for j in range(first, first + block)
        ]
        for n in range(block):
            j = first + n
            pivot = cols[n][j]
            inverse = 1.0 / pivot
            for i in range(j + 1, rank):
                ratio = cols[n][i] * inverse
                for k in range(n + 1, block):
                    cols[k][i] = cols[k][i] - ratio * cols[k][j]
                rows[i] = rows[i] - ratio * rows[j]
            table[j : j + 1, :] = (rows[j] * lax.rsqrt(pivot))[:1]
    return jnp.dot(table[:, rank : 2 * rank], factor, precision=HIGHEST, preferred_element_type=F32)


def kernel(
    outer, inner, chunks,
    grad, error, moment, start_dirs, norm_grads,
    own_approx, new_error, new_moment, mean_norm,
    grad_in, error_in, moment_in, dirs_in, norm_in, moment_out, error_out, inputs, swapped, high, low,
    norm_send, norm_recv, norm_part, norm_far,
    first_send, first_recv, factor_send, factor_recv, factor_all,
    dirs_send, dirs_recv, dirs_all, basis_own, basis_other, dirs_other, table,
    load_sem, store_sem, swap_ssem, swap_rsem, norm_ssem, norm_rsem, factor_ssem, factor_rsem, dirs_ssem, dirs_rsem,
):
    me, core = lax.axis_index("dp"), lax.axis_index("tensor")
    other = 1 - core
    far, near = lax.div(me, inner), lax.rem(me, inner)
    replicas = outer * inner
    rows, width = inputs.shape[1:]
    rank = dirs_in.shape[1]
    piece_rows = rows // chunks
    span = width // outer
    sends, stores = [], []

    def store(src, dst):
        copy = pltpu.make_async_copy(src, dst, store_sem.at[len(stores)])
        copy.start()
        stores.append(copy)

    def remote(src, dst, send_sem, recv_sem, to):
        return pltpu.make_async_remote_copy(
            src_ref=src, dst_ref=dst, send_sem=send_sem, recv_sem=recv_sem,
            device_id=to, device_id_type=pl.DeviceIdType.MESH,
        )

    def send(*args):
        copy = remote(*args)
        copy.start()
        sends.append(copy)
        return copy

    def near_at(d):
        return lax.rem(near + d + inner, inner)

    def far_at(d):
        return lax.rem(far + d + outer, outer)

    def near_peer(d):
        return (far * inner + near_at(d), core)

    def far_peer(d):
        return (far_at(d) * inner + near, core)

    def peer(d):
        return (lax.rem(me + d + replicas, replicas), core)

    def columns(z):
        return pl.ds(pl.multiple_of(z * span, span), span)

    last = 6 * chunks
    small = [
        pltpu.make_async_copy(src, dst, load_sem.at[last + k])
        for k, (src, dst) in enumerate(((start_dirs, dirs_in), (norm_grads, norm_in)))
    ]
    loads = []
    for i, m in enumerate((other, core)):
        for c in range(chunks):
            r = pl.ds(c * piece_rows, piece_rows)
            loads.append([
                pltpu.make_async_copy(src.at[0, m, r], dst.at[m, r], load_sem.at[(i * chunks + c) * 3 + k])
                for k, (src, dst) in enumerate(((grad, grad_in), (moment, moment_in), (error, error_in)))
            ])
    for n, group in enumerate(loads):
        for copy in group:
            copy.start()
        if n == 0:
            small[0].start()
            small[1].start()

    barrier = pltpu.get_barrier_semaphore()
    greeted = [peer(d) for d in range(1, replicas)] + [(me, other)]
    for device in greeted:
        pl.semaphore_signal(barrier, inc=1, device_id=device, device_id_type=pl.DeviceIdType.MESH)

    def form(i, m):
        for c in range(chunks):
            for copy in loads[i * chunks + c]:
                copy.wait()

            @pl.loop(0, piece_rows // 16)
            def _(g):
                r = pl.ds(pl.multiple_of(c * piece_rows + g * 16, 16), 16)
                moment_f = momentum_decay * moment_in[m, r, :].astype(F32) + grad_in[m, r, :].astype(F32)
                moment_out[m, r, :] = moment_f.astype(BF16)
                x = moment_f + error_in[m, r, :].astype(F32)
                inputs[m, r, :] = x
                high[m, r, :], low[m, r, :] = split(x)

        store(moment_out.at[m], new_moment.at[0, m])

    def left_of(dirs, h, cols=slice(None)):
        dirs_high, dirs_low = split(dirs)
        both = jnp.concatenate([dirs_high, dirs_low], axis=0)
        return dot_nt(high[h, :, cols], both), dot_nt(low[h, :, cols], dirs_high)

    def joined(wide, narrow):
        turned = wide.T
        return turned[:rank] + turned[rank:] + narrow.T

    def left_sum(step, factor, between=None):
        own, arrived, full = factor_send.at[step], factor_recv.at[step], factor_all.at[step]
        ssem, rsem = factor_ssem.at[step], factor_rsem.at[step]
        row_blocks = 2 * rows // LANES
        for j in range(replicas):
            a, b = divmod(j, row_blocks)
            own[j] = factor[a * SUBLANES : (a + 1) * SUBLANES, b * LANES : (b + 1) * LANES]
        order = sorted(range(1, replicas), key=lambda d: abs(2 * d - replicas))
        waits = [send(own.at[peer(d)[0]], arrived.at[d - 1], ssem.at[d - 1], rsem.at[d - 1], peer(d)) for d in order]
        if between is not None:
            between()
        for copy in waits:
            copy.wait_recv()
        total = own[me]
        for d in range(1, replicas):
            total = total + arrived[d - 1]
        full[me] = total
        base = replicas - 1
        for d in order:
            send(full.at[me], full.at[me], ssem.at[base + d - 1], rsem.at[base + d - 1], peer(d))
        for d in order:
            slot = full.at[peer(-d)[0]]
            remote(slot, slot, ssem.at[base + d - 1], rsem.at[base + d - 1], peer(d)).wait_recv()
        return jnp.concatenate(
            [
                jnp.concatenate([full[a * row_blocks + b] for b in range(row_blocks)], axis=1)
                for a in range(rank // SUBLANES)
            ],
            axis=0,
        )

    def right_sum(step, basis, consume):
        basis_high, basis_low = split(basis)
        both = jnp.concatenate([basis_high, basis_low], axis=0)
        own, arrived, full = dirs_send.at[step], dirs_recv.at[step], dirs_all.at[step]
        ssem, rsem = dirs_ssem.at[step], dirs_rsem.at[step]
        steps = [(dz, dq) for dz in list(range(1, outer)) + [0] for dq in range(inner) if dz or dq]
        waits = []

        def place(dz, dq):
            return (far_at(dz) * inner + near_at(dq), core)

        for dz in list(range(1, outer)) + [0]:
            z = far_at(dz)
            sums = low_sums = 0.0
            for h in range(2):
                half = slice(h * rows, (h + 1) * rows)
                sums += jnp.dot(both[:, half], high[h, :, columns(z)], preferred_element_type=F32)
                low_sums += jnp.dot(basis_high[:, half], low[h, :, columns(z)], preferred_element_type=F32)
            block = sums[:rank] + sums[rank:] + low_sums
            for q in range(inner):
                own[z, q] = block[:, q * LANES : (q + 1) * LANES]
            for dq in range(inner):
                if dz or dq:
                    k = dz * inner + dq - 1
                    waits.append(send(own.at[z, near_at(dq)], arrived.at[k], ssem.at[k], rsem.at[k], place(dz, dq)))
        for copy in waits:
            copy.wait_recv()
        total = own[far, near]
        for k in range(replicas - 1):
            total = total + arrived[k]
        full[far, near] = total
        base = replicas - 1
        for dz, dq in steps:
            k = base + dz * inner + dq - 1
            send(full.at[far, near], full.at[far, near], ssem.at[k], rsem.at[k], place(dz, dq))
        for dz in range(outer):
            z = far_at(-dz)
            for dq in range(inner):
                if dz or dq:
                    k = base + dz * inner + dq - 1
                    slot = full.at[z, near_at(-dq)]
                    remote(slot, slot, ssem.at[k], rsem.at[k], place(dz, dq)).wait_recv()
            consume(dz, z, jnp.concatenate([full[z, q] for q in range(inner)], axis=1))

    form(0, other)
    small[0].wait()
    first_send[...] = joined(*left_of(dirs_in[other], other))
    pl.semaphore_wait(barrier, len(greeted))
    first_swap = send(first_send, first_recv, swap_ssem.at[0], swap_rsem.at[0], (me, other))
    form(1, core)
    own_left = joined(*left_of(dirs_in[core], core))

    small[1].wait()
    gain_cols = mean_norm.shape[2]
    terms = norm_in[0].astype(F32)
    for z in range(outer):
        for q in range(inner):
            p = z * inner + q
            norm_send[q, z] = terms[:, p * gain_cols : (p + 1) * gain_cols]

    first_swap.wait_recv()
    their_left = first_recv[...]
    factor = jnp.concatenate([
        jnp.where(core == 0, own_left, their_left), jnp.where(core == 0, their_left, own_left)
    ], axis=1)

    norm_waits, norm_far_waits, matrix_swap = [], [], []

    def while_summing():
        for d in range(1, inner):
            norm_waits.append(send(norm_send.at[near_at(d)], norm_recv.at[d - 1], norm_ssem.at[d - 1], norm_rsem.at[d - 1], near_peer(d)))
        matrix_swap.append(send(inputs.at[other], swapped, swap_ssem.at[1], swap_rsem.at[1], (me, other)))

    basis = basis_of(left_sum(0, factor, while_summing), table)
    matrix_swap[0].wait_recv()

    @pl.loop(0, rows // 16)
    def _(g):
        r = pl.ds(pl.multiple_of(g * 16, 16), 16)
        high[other, r, :], low[other, r, :] = split(swapped[r, :])

    halves = [(0.0, 0.0), (0.0, 0.0)]

    def add_left(dz, z, block):
        for h in range(2):
            wide, narrow = left_of(block, h, columns(z))
            halves[h] = (halves[h][0] + wide, halves[h][1] + narrow)

    right_sum(0, basis, add_left)

    def norm_step():
        total = norm_send[near]
        for d in range(1, inner):
            norm_waits[d - 1].wait_recv()
            total = total + norm_recv[d - 1]
        norm_part[...] = total
        for d in range(1, outer):
            k = inner - 1 + d - 1
            norm_far_waits.append(send(norm_part.at[far_at(d)], norm_far.at[d - 1], norm_ssem.at[k], norm_rsem.at[k], far_peer(d)))

    basis = basis_of(left_sum(1, jnp.concatenate([joined(*half) for half in halves], axis=1), norm_step), table)
    basis_own[0], basis_own[1] = basis[:, :rows], basis[:, rows:]
    basis_swap = send(basis_own.at[other], basis_other, swap_ssem.at[2], swap_rsem.at[2], (me, other))

    def left_side(half):
        basis_high, basis_low = split(half)
        return jnp.concatenate([basis_high, basis_high, basis_low], axis=0).astype(F32).T.astype(BF16)

    def approx_of(lhs, block):
        dirs_high, dirs_low = split(block)
        rhs = jnp.concatenate([dirs_high, dirs_low, dirs_high], axis=0)
        return jnp.dot(lhs, rhs, preferred_element_type=F32) / replicas

    def finish(m, lhs, z, block):
        error_out[m, :, columns(z)] = (inputs[m, :, columns(z)] - approx_of(lhs, block)).astype(BF16)
        store(error_out.at[m, :, columns(z)], new_error.at[0, m, :, columns(z)])

    dirs_waits = []
    own_side = left_side(basis_own[core])

    def use_own(dz, z, block):
        k = 3 + dz
        dirs_waits.append(send(dirs_all.at[1, z], dirs_other.at[z], swap_ssem.at[k], swap_rsem.at[k], (me, other)))
        finish(core, own_side, z, block)

    right_sum(1, basis, use_own)
    own_approx[core] = approx_of(own_side, dirs_all[1, far, near])
    total = norm_part[far]
    for d in range(1, outer):
        norm_far_waits[d - 1].wait_recv()
        total = total + norm_far[d - 1]
    for m in range(2):
        mean_norm[m] = total[m : m + 1] / replicas
    basis_swap.wait_recv()
    other_side = left_side(basis_other[...])
    for dz in range(outer):
        z = far_at(-dz)
        dirs_waits[dz].wait_recv()
        finish(other, other_side, z, jnp.concatenate([dirs_other[z, q] for q in range(inner)], axis=1))
    own_approx[other] = approx_of(other_side, dirs_other[far, near])

    for copy in sends:
        copy.wait_send()
    for copy in stores:
        copy.wait()


def levels(replicas):
    near = max(d for d in range(1, replicas + 1) if replicas % d == 0 and d * d <= replicas)
    return replicas // near, near


def kernel_shards(grad_kv, error_kv, moment_kv, start_dirs, weight_kv, norm_grads, norm_gains):
    outer, inner = levels(lax.axis_size("dp"))
    _, matrices, rows, width = grad_kv.shape
    rank = start_dirs.shape[1]
    gain_cols = norm_gains.shape[2]
    chunks = 2
    hbm, vmem = pl.BlockSpec(memory_space=pltpu.HBM), pl.BlockSpec(memory_space=pltpu.VMEM)
    whole = (matrices, rows, width)
    dma = pltpu.SemaphoreType.DMA
    replicas = outer * inner
    sum_copies = 2 * (replicas - 1)
    tile = (SUBLANES, LANES)
    own_approx, new_error_kv, new_moment_kv, mean_norm = pl.pallas_call(
        functools.partial(kernel, outer, inner, chunks),
        out_shape=(
            jax.ShapeDtypeStruct(weight_kv.shape, F32),
            jax.ShapeDtypeStruct(error_kv.shape, BF16),
            jax.ShapeDtypeStruct(moment_kv.shape, BF16),
            jax.ShapeDtypeStruct(norm_gains.shape, F32),
        ),
        in_specs=[hbm] * 5,
        out_specs=(vmem, hbm, hbm, vmem),
        scratch_shapes=[
            pltpu.VMEM(whole, BF16), pltpu.VMEM(whole, BF16), pltpu.VMEM(whole, BF16),
            pltpu.VMEM(start_dirs.shape, F32), pltpu.VMEM(norm_grads.shape, BF16),
            pltpu.VMEM(whole, BF16), pltpu.VMEM(whole, BF16),
            pltpu.VMEM(whole, F32), pltpu.VMEM((rows, width), F32),
            pltpu.VMEM(whole, BF16), pltpu.VMEM(whole, BF16),
            pltpu.VMEM((inner, outer, matrices, gain_cols), F32), pltpu.VMEM((inner - 1, outer, matrices, gain_cols), F32),
            pltpu.VMEM((outer, matrices, gain_cols), F32), pltpu.VMEM((outer - 1, matrices, gain_cols), F32),
            pltpu.VMEM((rank, rows), F32), pltpu.VMEM((rank, rows), F32),
            pltpu.VMEM((2, replicas) + tile, F32), pltpu.VMEM((2, replicas - 1) + tile, F32),
            pltpu.VMEM((2, replicas) + tile, F32),
            pltpu.VMEM((2, outer, inner, rank, LANES), F32), pltpu.VMEM((2, replicas - 1, rank, LANES), F32),
            pltpu.VMEM((2, outer, inner, rank, LANES), F32),
            pltpu.VMEM((2, rank, rows), F32), pltpu.VMEM((rank, rows), F32),
            pltpu.VMEM((outer, inner, rank, LANES), F32), pltpu.VMEM((rank, LANES), F32),
            dma((6 * chunks + 2,)), dma((2 + 2 * outer,)), dma((3 + outer,)), dma((3 + outer,)),
            dma((inner + outer - 2,)), dma((inner + outer - 2,)),
            dma((2, sum_copies)), dma((2, sum_copies)), dma((2, sum_copies)), dma((2, sum_copies)),
        ],
        compiler_params=pltpu.CompilerParams(
            collective_id=0, has_side_effects=True, vmem_limit_bytes=48 * 2**20
        ),
        name="power_step",
    )(grad_kv, error_kv, moment_kv, start_dirs, norm_grads)
    new_weight_kv = weight_kv - step_size * own_approx
    new_gains = norm_gains - step_size * mean_norm
    return (new_weight_kv, new_error_kv, new_moment_kv, new_gains)


def solution(mesh):
    replicas, tensor = mesh.shape["dp"], mesh.shape["tensor"]

    def shards(*args):
        _, matrices, rows, width = args[0].shape
        rank = args[3].shape[1]
        _, near = levels(replicas)
        fits = (
            tensor == matrices == 2
            and near > 1
            and width == LANES * replicas
            and (rank // SUBLANES) * (2 * rows // LANES) == replicas
            and rank % SUBLANES == 0
            and rows % (2 * LANES) == 0
        )
        return (kernel_shards if fits else plain_shards)(*args)

    return jax.shard_map(
        shards,
        mesh=mesh,
        in_specs=(
            P("dp", None, "tensor", None),
            P("dp", None, "tensor", None),
            P("dp", None, "tensor", None),
            P(),
            P(None, "tensor", "dp"),
            P("dp", None, "tensor"),
            P(None, "tensor", "dp"),
        ),
        out_specs=(
            P(None, "tensor", "dp"),
            P("dp", None, "tensor", None),
            P("dp", None, "tensor", None),
            P(None, "tensor", "dp"),
        ),
        check_vma=False,
    )
```

```python
import functools

import jax
import jax.numpy as jnp
from jax import lax
from jax.experimental import pallas as pl
from jax.experimental.pallas import tpu as pltpu
from jax.sharding import PartitionSpec as P

momentum_decay = 0.9
step_size = 0.5
LANES = 128
SUBLANES = 8
F32 = jnp.float32
BF16 = jnp.bfloat16
HIGHEST = lax.Precision.HIGHEST


def project(inputs, directions):
    return jnp.einsum("mrd,mkd->mrk", inputs, directions, precision=HIGHEST)


def tri_solve(triangle, columns):
    return jax.scipy.linalg.solve_triangular(triangle, columns, lower=True)


def orthonormal(factor):
    full_rows = lax.all_gather(factor, "tensor", axis=1, tiled=True)
    gram_matrix = jnp.einsum("mrk,mrj->mkj", full_rows, full_rows, precision=HIGHEST)
    cholesky_factor = jnp.linalg.cholesky(gram_matrix)
    solved = jax.vmap(tri_solve)(cholesky_factor, jnp.swapaxes(factor, 1, 2))
    return jnp.swapaxes(solved, 1, 2)


def column_sums(inputs, basis):
    partial_sum = jnp.einsum("mrd,mrk->mkd", inputs, basis, precision=HIGHEST)
    return lax.psum(partial_sum, ("dp", "tensor"))


def plain_shards(grad_kv, error_kv, moment_kv, start_dirs, weight_kv, norm_grads, norm_gains):
    replicas = lax.axis_size("dp")
    dp_index = lax.axis_index("dp")
    moment_f = momentum_decay * moment_kv.astype(F32) + grad_kv.astype(F32)
    new_moment_kv = moment_f.astype(BF16)
    inputs = (moment_f + error_kv.astype(F32))[0]
    norm_terms = norm_grads[0].astype(F32)
    gain_cols = norm_gains.shape[2]
    factor = project(inputs, start_dirs)
    factor, norm_total = lax.psum((factor, norm_terms), "dp")
    own_norm = lax.dynamic_slice_in_dim(norm_total, dp_index * gain_cols, gain_cols, 1)
    mean_norm = own_norm / replicas
    basis = orthonormal(factor)
    directions = column_sums(inputs, basis)
    factor = lax.psum(project(inputs, directions), "dp")
    basis = orthonormal(factor)
    directions = column_sums(inputs, basis)
    approx = jnp.einsum("mrk,mkd->mrd", basis, directions, precision=HIGHEST) / replicas
    new_error_kv = (inputs - approx).astype(BF16)[None]
    weight_cols = weight_kv.shape[2]
    own_approx = lax.dynamic_slice_in_dim(approx, dp_index * weight_cols, weight_cols, 2)
    new_weight_kv = weight_kv - step_size * own_approx
    new_gains = norm_gains - step_size * mean_norm[:, None, :]
    return (new_weight_kv, new_error_kv, new_moment_kv, new_gains)


def split(value):
    high = value.astype(BF16)
    return high, (value - high.astype(F32)).astype(BF16)


def dot_nt(a, b):
    return lax.dot_general(a, b, (((1,), (1,)), ((), ())), preferred_element_type=F32)


def basis_of(factor, table, block=4):
    rank = factor.shape[0]
    gram = lax.dot_general(
        factor, factor, (((1,), (1,)), ((), ())), precision=HIGHEST, preferred_element_type=F32
    )
    shape = (SUBLANES, LANES)
    lane = lax.broadcasted_iota(jnp.int32, (rank, LANES), 1)
    line = lax.broadcasted_iota(jnp.int32, (rank, LANES), 0)
    table[...] = jnp.concatenate([gram, (lane == line + rank).astype(F32)[:, rank:]], axis=1)
    rows = [jnp.broadcast_to(table[i : i + 1, :], shape) for i in range(rank)]
    for first in range(0, rank, block):
        cols = [
            {i: jnp.broadcast_to(rows[i][:, j : j + 1], shape) for i in range(first, rank)}
            for j in range(first, first + block)
        ]
        for n in range(block):
            j = first + n
            pivot = cols[n][j]
            inverse = 1.0 / pivot
            for i in range(j + 1, rank):
                ratio = cols[n][i] * inverse
                for k in range(n + 1, block):
                    cols[k][i] = cols[k][i] - ratio * cols[k][j]
                rows[i] = rows[i] - ratio * rows[j]
            table[j : j + 1, :] = (rows[j] * lax.rsqrt(pivot))[:1]
    return jnp.dot(table[:, rank : 2 * rank], factor, precision=HIGHEST, preferred_element_type=F32)


def kernel(
    outer, inner, chunks,
    grad, error, moment, start_dirs, norm_grads,
    own_approx, new_error, new_moment, mean_norm,
    grad_in, error_in, moment_in, dirs_in, norm_in, moment_out, error_out, inputs, swapped, high, low,
    norm_send, norm_recv, norm_part, norm_far,
    first_send, first_recv, factor_send, factor_recv, factor_all,
    dirs_send, dirs_recv, dirs_all, basis_own, basis_other, dirs_other, table,
    first_ssem, first_rsem, load_sem, store_sem, swap_ssem, swap_rsem, norm_ssem, norm_rsem, factor_ssem, factor_rsem, dirs_ssem, dirs_rsem,
):
    me, core = lax.axis_index("dp"), lax.axis_index("tensor")
    other = 1 - core
    far, near = lax.div(me, inner), lax.rem(me, inner)
    replicas = outer * inner
    rows, width = inputs.shape[1:]
    rank = dirs_in.shape[1]
    piece_rows = rows // chunks
    span = width // outer
    sends, stores = [], []

    def store(src, dst):
        copy = pltpu.make_async_copy(src, dst, store_sem.at[len(stores)])
        copy.start()
        stores.append(copy)

    def remote(src, dst, send_sem, recv_sem, to):
        return pltpu.make_async_remote_copy(
            src_ref=src, dst_ref=dst, send_sem=send_sem, recv_sem=recv_sem,
            device_id=to, device_id_type=pl.DeviceIdType.MESH,
        )

    def send(*args):
        copy = remote(*args)
        copy.start()
        sends.append(copy)
        return copy

    def near_at(d):
        return lax.rem(near + d + inner, inner)

    def far_at(d):
        return lax.rem(far + d + outer, outer)

    def near_peer(d):
        return (far * inner + near_at(d), core)

    def far_peer(d):
        return (far_at(d) * inner + near, core)

    def peer(d):
        return (lax.rem(me + d + replicas, replicas), core)

    def columns(z):
        return pl.ds(pl.multiple_of(z * span, span), span)

    last = 6 * chunks
    small = [
        pltpu.make_async_copy(src, dst, load_sem.at[last + k])
        for k, (src, dst) in enumerate(((start_dirs, dirs_in), (norm_grads, norm_in)))
    ]
    loads = []
    for i, m in enumerate((other, core)):
        for c in range(chunks):
            r = pl.ds(c * piece_rows, piece_rows)
            loads.append([
                pltpu.make_async_copy(src.at[0, m, r], dst.at[m, r], load_sem.at[(i * chunks + c) * 3 + k])
                for k, (src, dst) in enumerate(((grad, grad_in), (moment, moment_in), (error, error_in)))
            ])
    for n, group in enumerate(loads):
        for copy in group:
            copy.start()
        if n == 0:
            small[0].start()
            small[1].start()

    barrier = pltpu.get_barrier_semaphore()
    greeted = [(peer(d)[0], c) for d in range(1, replicas) for c in (core, other)] + [(me, other)]
    for device in greeted:
        pl.semaphore_signal(barrier, inc=1, device_id=device, device_id_type=pl.DeviceIdType.MESH)

    def form(i, m):
        for c in range(chunks):
            for copy in loads[i * chunks + c]:
                copy.wait()

            @pl.loop(0, piece_rows // 16)
            def _(g):
                r = pl.ds(pl.multiple_of(c * piece_rows + g * 16, 16), 16)
                moment_f = momentum_decay * moment_in[m, r, :].astype(F32) + grad_in[m, r, :].astype(F32)
                moment_out[m, r, :] = moment_f.astype(BF16)
                x = moment_f + error_in[m, r, :].astype(F32)
                inputs[m, r, :] = x
                high[m, r, :], low[m, r, :] = split(x)

        store(moment_out.at[m], new_moment.at[0, m])

    def left_of(dirs, h, cols=slice(None)):
        dirs_high, dirs_low = split(dirs)
        both = jnp.concatenate([dirs_high, dirs_low], axis=0)
        return dot_nt(high[h, :, cols], both), dot_nt(low[h, :, cols], dirs_high)

    def joined(wide, narrow):
        turned = wide.T
        return turned[:rank] + turned[rank:] + narrow.T

    row_blocks = 2 * rows // LANES
    half_blocks = row_blocks // 2
    far_first = sorted(range(1, replicas), key=lambda d: abs(2 * d - replicas))
    own_tiles = [(a, b) for a in range(rank // SUBLANES) for b in range(half_blocks)]
    first_waits = []

    def first_scatter(i, m, factor):
        for n, (a, b) in enumerate(own_tiles):
            j = a * row_blocks + core * half_blocks + b
            k = i * len(own_tiles) + n
            first_send[k] = factor[a * SUBLANES : (a + 1) * SUBLANES, b * LANES : (b + 1) * LANES]
            copy = remote(first_send.at[k], first_recv.at[me], first_ssem.at[k], first_rsem.at[me], (j, m))
            if i == 0:
                copy.start()
                sends.append(copy)
            else:
                pl.when(j != me)(copy.start)
                first_waits.append((j, copy))

                @pl.when(j == me)
                def _():
                    first_recv[me] = first_send[k]

    def first_sum():
        here = lax.div(lax.rem(me, row_blocks), half_blocks) == core
        for n in range(replicas):
            slot = first_recv.at[n]
            copy = remote(slot, slot, first_ssem.at[0], first_rsem.at[n], (me, other))
            pl.when(jnp.logical_not(jnp.logical_and(here, me == n)))(copy.wait_recv)
        total = first_recv[0]
        for n in range(1, replicas):
            total = total + first_recv[n]
        return left_spread(0, total)

    def left_spread(step, total):
        full, ssem, rsem = factor_all.at[step], factor_ssem.at[step], factor_rsem.at[step]
        full[me] = total
        base = replicas - 1
        for d in far_first:
            send(full.at[me], full.at[me], ssem.at[base + d - 1], rsem.at[base + d - 1], peer(d))
        for d in far_first:
            slot = full.at[peer(-d)[0]]
            remote(slot, slot, ssem.at[base + d - 1], rsem.at[base + d - 1], peer(d)).wait_recv()
        return jnp.concatenate(
            [
                jnp.concatenate([full[a * row_blocks + b] for b in range(row_blocks)], axis=1)
                for a in range(rank // SUBLANES)
            ],
            axis=0,
        )

    def left_sum(factor, between):
        own, arrived = factor_send.at[1], factor_recv.at[1]
        ssem, rsem = factor_ssem.at[1], factor_rsem.at[1]
        for j in range(replicas):
            a, b = divmod(j, row_blocks)
            own[j] = factor[a * SUBLANES : (a + 1) * SUBLANES, b * LANES : (b + 1) * LANES]
        waits = [send(own.at[peer(d)[0]], arrived.at[d - 1], ssem.at[d - 1], rsem.at[d - 1], peer(d)) for d in far_first]
        between()
        for copy in waits:
            copy.wait_recv()
        total = own[me]
        for d in range(1, replicas):
            total = total + arrived[d - 1]
        return left_spread(1, total)

    def right_sum(step, basis, consume):
        basis_high, basis_low = split(basis)
        both = jnp.concatenate([basis_high, basis_low], axis=0)
        own, arrived, full = dirs_send.at[step], dirs_recv.at[step], dirs_all.at[step]
        ssem, rsem = dirs_ssem.at[step], dirs_rsem.at[step]
        steps = [(dz, dq) for dz in list(range(1, outer)) + [0] for dq in range(inner) if dz or dq]
        waits = []

        def place(dz, dq):
            return (far_at(dz) * inner + near_at(dq), core)

        for dz in list(range(1, outer)) + [0]:
            z = far_at(dz)
            sums = low_sums = 0.0
            for h in range(2):
                half = slice(h * rows, (h + 1) * rows)
                sums += jnp.dot(both[:, half], high[h, :, columns(z)], preferred_element_type=F32)
                low_sums += jnp.dot(basis_high[:, half], low[h, :, columns(z)], preferred_element_type=F32)
            block = sums[:rank] + sums[rank:] + low_sums
            for q in range(inner):
                own[z, q] = block[:, q * LANES : (q + 1) * LANES]
            for dq in range(inner):
                if dz or dq:
                    k = dz * inner + dq - 1
                    waits.append(send(own.at[z, near_at(dq)], arrived.at[k], ssem.at[k], rsem.at[k], place(dz, dq)))
        for copy in waits:
            copy.wait_recv()
        total = own[far, near]
        for k in range(replicas - 1):
            total = total + arrived[k]
        full[far, near] = total
        base = replicas - 1
        for dz, dq in steps:
            k = base + dz * inner + dq - 1
            send(full.at[far, near], full.at[far, near], ssem.at[k], rsem.at[k], place(dz, dq))
        for dz in range(outer):
            z = far_at(-dz)
            for dq in range(inner):
                if dz or dq:
                    k = base + dz * inner + dq - 1
                    slot = full.at[z, near_at(-dq)]
                    remote(slot, slot, ssem.at[k], rsem.at[k], place(dz, dq)).wait_recv()
            consume(dz, z, jnp.concatenate([full[z, q] for q in range(inner)], axis=1))

    form(0, other)
    small[0].wait()
    their_left = joined(*left_of(dirs_in[other], other))
    pl.semaphore_wait(barrier, len(greeted))
    first_scatter(0, other, their_left)
    form(1, core)
    first_scatter(1, core, joined(*left_of(dirs_in[core], core)))
    matrix_swap = send(inputs.at[other], swapped, swap_ssem.at[1], swap_rsem.at[1], (me, other))

    small[1].wait()
    gain_cols = mean_norm.shape[2]
    terms = norm_in[0].astype(F32)
    for z in range(outer):
        for q in range(inner):
            p = z * inner + q
            norm_send[q, z] = terms[:, p * gain_cols : (p + 1) * gain_cols]

    norm_waits, norm_far_waits = [], []
    for d in range(1, inner):
        norm_waits.append(send(norm_send.at[near_at(d)], norm_recv.at[d - 1], norm_ssem.at[d - 1], norm_rsem.at[d - 1], near_peer(d)))
    basis = basis_of(first_sum(), table)
    matrix_swap.wait_recv()

    @pl.loop(0, rows // 16)
    def _(g):
        r = pl.ds(pl.multiple_of(g * 16, 16), 16)
        high[other, r, :], low[other, r, :] = split(swapped[r, :])

    halves = [(0.0, 0.0), (0.0, 0.0)]

    def add_left(dz, z, block):
        for h in range(2):
            wide, narrow = left_of(block, h, columns(z))
            halves[h] = (halves[h][0] + wide, halves[h][1] + narrow)

    right_sum(0, basis, add_left)

    def norm_step():
        total = norm_send[near]
        for d in range(1, inner):
            norm_waits[d - 1].wait_recv()
            total = total + norm_recv[d - 1]
        norm_part[...] = total
        for d in range(1, outer):
            k = inner - 1 + d - 1
            norm_far_waits.append(send(norm_part.at[far_at(d)], norm_far.at[d - 1], norm_ssem.at[k], norm_rsem.at[k], far_peer(d)))

    basis = basis_of(left_sum(jnp.concatenate([joined(*half) for half in halves], axis=1), norm_step), table)
    basis_own[0], basis_own[1] = basis[:, :rows], basis[:, rows:]
    basis_swap = send(basis_own.at[other], basis_other, swap_ssem.at[2], swap_rsem.at[2], (me, other))

    def left_side(half):
        basis_high, basis_low = split(half)
        return jnp.concatenate([basis_high, basis_high, basis_low], axis=0).astype(F32).T.astype(BF16)

    def approx_of(lhs, block):
        dirs_high, dirs_low = split(block)
        rhs = jnp.concatenate([dirs_high, dirs_low, dirs_high], axis=0)
        return jnp.dot(lhs, rhs, preferred_element_type=F32) / replicas

    def finish(m, lhs, z, block):
        error_out[m, :, columns(z)] = (inputs[m, :, columns(z)] - approx_of(lhs, block)).astype(BF16)
        store(error_out.at[m, :, columns(z)], new_error.at[0, m, :, columns(z)])

    dirs_waits = []
    own_side = left_side(basis_own[core])

    def use_own(dz, z, block):
        k = 3 + dz
        dirs_waits.append(send(dirs_all.at[1, z], dirs_other.at[z], swap_ssem.at[k], swap_rsem.at[k], (me, other)))
        finish(core, own_side, z, block)

    right_sum(1, basis, use_own)
    own_approx[core] = approx_of(own_side, dirs_all[1, far, near])
    total = norm_part[far]
    for d in range(1, outer):
        norm_far_waits[d - 1].wait_recv()
        total = total + norm_far[d - 1]
    for m in range(2):
        mean_norm[m] = total[m : m + 1] / replicas
    basis_swap.wait_recv()
    other_side = left_side(basis_other[...])
    for dz in range(outer):
        z = far_at(-dz)
        dirs_waits[dz].wait_recv()
        finish(other, other_side, z, jnp.concatenate([dirs_other[z, q] for q in range(inner)], axis=1))
    own_approx[other] = approx_of(other_side, dirs_other[far, near])

    for copy in sends:
        copy.wait_send()
    for j, copy in first_waits:
        pl.when(j != me)(copy.wait_send)
    for copy in stores:
        copy.wait()


def levels(replicas):
    near = max(d for d in range(1, replicas + 1) if replicas % d == 0 and d * d <= replicas)
    return replicas // near, near


def kernel_shards(grad_kv, error_kv, moment_kv, start_dirs, weight_kv, norm_grads, norm_gains):
    outer, inner = levels(lax.axis_size("dp"))
    _, matrices, rows, width = grad_kv.shape
    rank = start_dirs.shape[1]
    gain_cols = norm_gains.shape[2]
    chunks = 2
    hbm, vmem = pl.BlockSpec(memory_space=pltpu.HBM), pl.BlockSpec(memory_space=pltpu.VMEM)
    whole = (matrices, rows, width)
    dma = pltpu.SemaphoreType.DMA
    replicas = outer * inner
    sum_copies = 2 * (replicas - 1)
    tile = (SUBLANES, LANES)
    own_approx, new_error_kv, new_moment_kv, mean_norm = pl.pallas_call(
        functools.partial(kernel, outer, inner, chunks),
        out_shape=(
            jax.ShapeDtypeStruct(weight_kv.shape, F32),
            jax.ShapeDtypeStruct(error_kv.shape, BF16),
            jax.ShapeDtypeStruct(moment_kv.shape, BF16),
            jax.ShapeDtypeStruct(norm_gains.shape, F32),
        ),
        in_specs=[hbm] * 5,
        out_specs=(vmem, hbm, hbm, vmem),
        scratch_shapes=[
            pltpu.VMEM(whole, BF16), pltpu.VMEM(whole, BF16), pltpu.VMEM(whole, BF16),
            pltpu.VMEM(start_dirs.shape, F32), pltpu.VMEM(norm_grads.shape, BF16),
            pltpu.VMEM(whole, BF16), pltpu.VMEM(whole, BF16),
            pltpu.VMEM(whole, F32), pltpu.VMEM((rows, width), F32),
            pltpu.VMEM(whole, BF16), pltpu.VMEM(whole, BF16),
            pltpu.VMEM((inner, outer, matrices, gain_cols), F32), pltpu.VMEM((inner - 1, outer, matrices, gain_cols), F32),
            pltpu.VMEM((outer, matrices, gain_cols), F32), pltpu.VMEM((outer - 1, matrices, gain_cols), F32),
            pltpu.VMEM((replicas,) + tile, F32), pltpu.VMEM((replicas,) + tile, F32),
            pltpu.VMEM((2, replicas) + tile, F32), pltpu.VMEM((2, replicas - 1) + tile, F32),
            pltpu.VMEM((2, replicas) + tile, F32),
            pltpu.VMEM((2, outer, inner, rank, LANES), F32), pltpu.VMEM((2, replicas - 1, rank, LANES), F32),
            pltpu.VMEM((2, outer, inner, rank, LANES), F32),
            pltpu.VMEM((2, rank, rows), F32), pltpu.VMEM((rank, rows), F32),
            pltpu.VMEM((outer, inner, rank, LANES), F32), pltpu.VMEM((rank, LANES), F32),
            dma((replicas,)), dma((replicas,)), dma((6 * chunks + 2,)), dma((2 + 2 * outer,)), dma((3 + outer,)), dma((3 + outer,)),
            dma((inner + outer - 2,)), dma((inner + outer - 2,)),
            dma((2, sum_copies)), dma((2, sum_copies)), dma((2, sum_copies)), dma((2, sum_copies)),
        ],
        compiler_params=pltpu.CompilerParams(
            collective_id=0, has_side_effects=True, vmem_limit_bytes=48 * 2**20
        ),
        name="power_step",
    )(grad_kv, error_kv, moment_kv, start_dirs, norm_grads)
    new_weight_kv = weight_kv - step_size * own_approx
    new_gains = norm_gains - step_size * mean_norm
    return (new_weight_kv, new_error_kv, new_moment_kv, new_gains)


def solution(mesh):
    replicas, tensor = mesh.shape["dp"], mesh.shape["tensor"]

    def shards(*args):
        _, matrices, rows, width = args[0].shape
        rank = args[3].shape[1]
        _, near = levels(replicas)
        fits = (
            tensor == matrices == 2
            and near > 1
            and width == LANES * replicas
            and (rank // SUBLANES) * (2 * rows // LANES) == replicas
            and rank % SUBLANES == 0
            and rows % (2 * LANES) == 0
        )
        return (kernel_shards if fits else plain_shards)(*args)

    return jax.shard_map(
        shards,
        mesh=mesh,
        in_specs=(
            P("dp", None, "tensor", None),
            P("dp", None, "tensor", None),
            P("dp", None, "tensor", None),
            P(),
            P(None, "tensor", "dp"),
            P("dp", None, "tensor"),
            P(None, "tensor", "dp"),
        ),
        out_specs=(
            P(None, "tensor", "dp"),
            P("dp", None, "tensor", None),
            P("dp", None, "tensor", None),
            P(None, "tensor", "dp"),
        ),
        check_vma=False,
    )
```
